32 devices in a mesh: dp: 8 (over y, x, core), mp: 4 (over z).
Axes of the slice: x: 2, y: 2, z: 4, core: 2. Of those that a mesh axis runs over, the one named last changes fastest.
Arguments:
- tokens: bfloat16 [8192, 2048], P(('dp', 'mp')), may hold values from -6 to 6
- input_gain: float32 [2048], replicated, may hold values from 0.5 to 1.5
- query_weight: bfloat16 [2048, 4096], P('dp', 'mp'), may hold values from -0.125 to 0.125
- key_value_weight: bfloat16 [2048, 1024], P('dp'), may hold values from -0.125 to 0.125
- query_gain: float32 [128], replicated, may hold values from 0.5 to 1.5
- key_gain: float32 [128], replicated, may hold values from 0.5 to 1.5
- out_weight: bfloat16 [4096, 2048], P('mp', 'dp'), may hold values from -0.75 to 0.75
- moe_gain: float32 [2048], replicated, may hold values from 0.5 to 1.5
- gate_weight: bfloat16 [32, 2048, 768], P(('dp', 'mp')), may hold values from -0.125 to 0.125
- up_weight: bfloat16 [32, 2048, 768], P(('dp', 'mp')), may hold values from -0.125 to 0.125
- down_weight: bfloat16 [32, 768, 2048], P(('dp', 'mp')), may hold values from -0.875 to 0.875
- gate_values: float32 [8192, 8], P(('dp', 'mp')), may hold values from 0 to 1, as said below
- routes: int32 [8192, 8], P(('dp', 'mp')), may hold values from 0 to 31, all different within a row; in each aligned block of 256 rows (0 to 255, 256 to 511, ...) at most 68 rows name the same one
- lengths: int32 [4, 4], replicated, may hold values from 1 to 1536, 2048 in all within a row
- cotangent: bfloat16 [8192, 2048], P(('dp', 'mp')), may hold values from -6 to 6
Outputs:
- block_out: bfloat16 [8192, 2048], P(('dp', 'mp'))
- tokens_grad: float32 [8192, 2048], P(('dp', 'mp'))
- input_gain_grad: float32 [2048], replicated
- query_weight_grad: float32 [2048, 4096], P('dp', 'mp')
- kv_weight_grad: float32 [2048, 1024], P('dp')
- query_gain_grad: float32 [128], replicated
- key_gain_grad: float32 [128], replicated
- out_weight_grad: float32 [4096, 2048], P('mp', 'dp')
- moe_gain_grad: float32 [2048], replicated
- gate_weight_grad: float32 [32, 2048, 768], P(('dp', 'mp'))
- up_weight_grad: float32 [32, 2048, 768], P(('dp', 'mp'))
- down_weight_grad: float32 [32, 768, 2048], P(('dp', 'mp'))
- gate_values_grad: float32 [8192, 8], P(('dp', 'mp'))
The draws below stay inside these ranges and needn't reach their ends.
Inputs may be any that keep to these rules, and one draw needn't show every extreme that they name: `routes`: each row names 8 different experts; in the rows of one device (aligned blocks of 256 rows) no expert is named by more than 68 rows, a bound that some block reaches. `gate_values`: each row's 8 weights are positive and sum to 1. Each sequence's 4 lengths sum to 2048; the longest is exactly 1536.
All inputs are finite; a program needn't handle non-finite values.
Results may differ from the reference program's by a relative error of at most 0.02.
Values may be sent and summed in bfloat16 or wider, within the bound.
No kernel may reach another device: no remote copies, remote signals or barrier semaphores. Data moves between devices by JAX's collectives and lax.ppermute only.
A program may use at most 320 MiB of HBM per device.

```python
import math
import jax
import jax.numpy as jnp
import numpy as np
from jax import lax

MODEL_DIM = 2048
QUERY_HEADS = 32
KEY_VALUE_HEADS = 4
HEAD_SIZE = 128
FF = 768
TOP = 8
WINDOW = 1024
DOCS = 4
TOK_DEV = 1024
ROWS = 256
SEQS = 4
TOKENS = 8192
EXPERTS = 32
CAP = 68
N_DP = 8
N_MP = 4


def draw_gate_values(key, part):
    key = jax.random.fold_in(key, 11)
    logits = 0.5 * jax.random.normal(key, (TOKENS, TOP), jnp.float32)
    weights = jnp.exp(logits)
    return weights / jnp.sum(weights, axis=-1, keepdims=True)


def block_levels(own_key, extent, pieces, least, largest):
    gain, own = 1.0, jax.random.fold_in(own_key, 6)
    for axis_at, parts in pieces:
        draws = jnp.exp(jax.random.uniform(jax.random.fold_in(own, axis_at), (parts,), jnp.float32, least / len(pieces), largest / len(pieces)))
        gain = gain * jnp.repeat(draws, extent[axis_at] // parts).reshape([-1 if axis == axis_at else 1 for axis in range(len(extent))])
    return gain


def profile(count, total, bound, skew):
    loads = [(1 << 20) // math.isqrt(rank ** skew) + 1 for rank in range(2, count + 1)]
    rest, given = total - bound - (count - 1), [1] * (count - 1)
    while rest > 0:
        candidates = [i for i in range(count - 1) if given[i] < bound]
        pool, budget = sum([loads[i] for i in candidates]), rest
        for i in candidates:
            more = min(bound - given[i], max(1, budget * loads[i] // pool), rest)
            given[i] = given[i] + more
            rest = rest - more
    return np.array([bound] + given)


def uneven(own_key, number_of, total, most, lean):
    if number_of == 2:
        one = jax.random.randint(own_key, (), max(1, total - most), min(most, total - 1) + 1)
        return jnp.stack([one, total - one])
    tallies = jnp.asarray(profile(number_of, total, most, lean), jnp.int32)
    couples = (number_of - 1) // 2
    source_of, sink = tallies[1:1 + 2 * couples:2], tallies[2:2 + 2 * couples:2]
    room = jnp.minimum(source_of - 1, most - sink)
    moved = jax.random.randint(jax.random.fold_in(own_key, 1), (couples,), 0, 1 << 20) % (room + 1)
    tallies = tallies.at[1:1 + 2 * couples:2].set(source_of - moved).at[2:2 + 2 * couples:2].set(sink + moved)
    return tallies[jax.random.permutation(jax.random.fold_in(own_key, 2), number_of)]


def assign_block(rng, own, number, rows, count, top, most, slope):
    sequence = jax.random.permutation(rng, count)
    packed, ordinary = load_shares(count, rows * top, most, slope, True), load_shares(count, rows * top, most, slope, False)
    places = jnp.arange(count)

    def named(sizes, turn):
        used = int((sizes > 0).sum())
        fixed = max(1, used // 4)
        moved = fixed + (places - fixed + turn * (used - fixed)) % max(1, count - fixed)
        return jnp.zeros((count,), jnp.int32).at[sequence[jnp.where(places < fixed, places, moved)]].set(jnp.asarray(sizes, jnp.int32))

    sizes = jnp.where(number % 4 == 0, named(packed, number // 4), named(ordinary, number - number // 4 - 1))
    mixed = jax.random.permutation(jax.random.fold_in(own, 3), count)
    source_of, sink = mixed[0:count // 2 * 2:2], mixed[1:count // 2 * 2:2]
    margin = jnp.minimum(sizes[source_of] - 1, most - sizes[sink]) // 2
    margin = jnp.where((source_of == sequence[0]) | (sink == sequence[0]) | (sizes[sink] == 0), 0, jnp.maximum(margin, 0))
    moved = jax.random.randint(jax.random.fold_in(own, 4), (count // 2,), 0, 1 << 20) % (margin + 1)
    sizes = sizes.at[source_of].add(-moved).at[sink].add(moved)
    items = jnp.searchsorted(jnp.cumsum(sizes), jnp.arange(rows * top), side="right").astype(jnp.int32)
    listing = items.reshape(top, rows).T
    listing = listing[jax.random.permutation(jax.random.fold_in(own, 1), rows)]
    turn = jax.random.randint(jax.random.fold_in(own, 2), (rows, 1), 0, top)
    return jnp.take_along_axis(listing, (jnp.arange(top)[None, :] + turn) % top, axis=1)


def load_shares(amount, total, reach, lean, full):
    portions = [(1 << 20) // math.isqrt(rank ** lean) + 1 for rank in range(1, amount + 1)]
    largest = reach if full else min(reach, max(-(-total // amount), total * portions[0] // sum(portions)))
    least = 1 if total - largest >= amount - 1 else 0
    holding, surplus = [largest] + [least] * (amount - 1), total - largest - least * (amount - 1)
    while surplus > 0:
        free = [i for i in range(1, amount) if holding[i] < largest] or [i for i in range(1, amount) if holding[i] < reach]
        pool, left = sum([portions[i] for i in free]), surplus
        for i in free:
            more = min(reach - holding[i], max(1, left * portions[i] // pool), surplus)
            holding[i] = holding[i] + more
            surplus = surplus - more
    return np.array(holding)


def centred(key, extent, deviation, limit, split=(), kind=jnp.bfloat16):
    array = deviation * jax.random.normal(key, extent, jnp.float32)
    if split:
        array = array * block_levels(key, extent, split, -0.22, 0.18)
    return jnp.clip(array, -limit, limit).astype(kind)


def setup_inputs(seed: int = 0) -> dict:
    key_of = jax.random.split(jax.random.key(seed), 16)
    tokens = centred(key_of[0], (TOKENS, MODEL_DIM), 1.0, 6.0, ((0, 32),))
    input_gain = jnp.clip(1.0 + 0.1 * jax.random.normal(key_of[1], (MODEL_DIM,), jnp.float32), 0.5, 1.5)
    query_weight = centred(key_of[2], (MODEL_DIM, QUERY_HEADS * HEAD_SIZE), MODEL_DIM ** -0.5, 0.125, ((0, 8), (1, 4)))
    key_value_weight = centred(key_of[3], (MODEL_DIM, 2 * KEY_VALUE_HEADS * HEAD_SIZE), MODEL_DIM ** -0.5, 0.125, ((0, 8),))
    query_gain = jnp.clip(1.0 + 0.1 * jax.random.normal(key_of[4], (HEAD_SIZE,), jnp.float32), 0.5, 1.5)
    key_gain = jnp.clip(1.0 + 0.1 * jax.random.normal(key_of[5], (HEAD_SIZE,), jnp.float32), 0.5, 1.5)
    out_weight = centred(key_of[6], (QUERY_HEADS * HEAD_SIZE, MODEL_DIM), (QUERY_HEADS * HEAD_SIZE // 64) ** -0.5, 0.75, ((0, 4), (1, 8)))
    moe_gain = jnp.clip(1.0 + 0.1 * jax.random.normal(key_of[7], (MODEL_DIM,), jnp.float32), 0.5, 1.5)
    gate_weight = centred(key_of[8], (EXPERTS, MODEL_DIM, FF), MODEL_DIM ** -0.5, 0.125, ((0, 32),))
    up_weight = centred(key_of[9], (EXPERTS, MODEL_DIM, FF), MODEL_DIM ** -0.5, 0.125, ((0, 32),))
    down_weight = centred(key_of[10], (EXPERTS, FF, MODEL_DIM), (FF // 16) ** -0.5, 0.875, ((0, 32),))
    gate_values = draw_gate_values(jax.random.fold_in(key_of[15], 71), 0)
    routes_keys = jax.random.split(jax.random.fold_in(key_of[12], 1), TOKENS // ROWS)
    routes_turns = jax.random.permutation(jax.random.fold_in(key_of[12], 3), TOKENS // ROWS)
    routes = jax.vmap(lambda own, number: assign_block(jax.random.fold_in(key_of[12], 2), own, number, ROWS, EXPERTS, TOP, CAP, 0))(routes_keys, routes_turns).reshape((TOKENS, TOP))
    lengths = jax.vmap(lambda own: uneven(own, DOCS, 2 * TOK_DEV, 2 * TOK_DEV - 2 * TOK_DEV // 4, 2))(jax.random.split(key_of[13], SEQS)).reshape((SEQS, DOCS)).astype(jnp.int32)
    cotangent = centred(key_of[14], (TOKENS, MODEL_DIM), 1.0, 6.0, ((0, 32),))
    return dict(tokens=tokens, input_gain=input_gain, query_weight=query_weight, key_value_weight=key_value_weight, query_gain=query_gain, key_gain=key_gain, out_weight=out_weight, moe_gain=moe_gain, gate_weight=gate_weight, up_weight=up_weight, down_weight=down_weight, gate_values=gate_values, routes=routes, lengths=lengths, cotangent=cotangent)


EPSILON = 1e-06
ROPE_BASE = 1000000.0
MASKED = -1e+30
HIGHEST = lax.Precision.HIGHEST

@jax.custom_vjp
def low(v):
    return lax.optimization_barrier(v.astype(jnp.bfloat16)).astype(jnp.float32)

@jax.custom_vjp
def low_back(v):
    return v

def low_keep(v):
    return (low(v), None)

def low_pass(kept, grad):
    return (grad,)

def back_keep(v):
    return (v, None)

def back_low(kept, grad):
    return (low(grad),)
low.defvjp(low_keep, low_pass)
low_back.defvjp(back_keep, back_low)

def rms_norm(value_rows, gain_vector):
    return value_rows * lax.rsqrt(lax.optimization_barrier(jnp.mean(value_rows * value_rows, axis=-1, keepdims=True)) + EPSILON) * gain_vector

def product(left_side, right_side):
    return jnp.dot(left_side, right_side, precision=HIGHEST)

def rope_tables(positions, head_width):
    half_width = head_width // 2
    frequency = jnp.exp(jnp.arange(half_width, dtype=jnp.float32) * (-2.0 * math.log(ROPE_BASE) / head_width))
    angles = positions[:, None] * frequency[None, :]
    cosine = jnp.cos(angles)
    sine_table = jnp.sin(angles)
    return (jnp.concatenate([cosine, cosine], axis=-1), jnp.concatenate([sine_table, sine_table], axis=-1))

def rotate(value_rows, cosine, sine_table):
    half_width = value_rows.shape[-1] // 2
    turned = jnp.concatenate([-value_rows[..., half_width:], value_rows[..., :half_width]], axis=-1)
    return value_rows * cosine[:, None, :] + turned * sine_table[:, None, :]

def doc_layout(doc_lengths, sequence_length):
    ends_at = jnp.cumsum(doc_lengths).astype(jnp.int32)
    starts_at = ends_at - doc_lengths
    places = jnp.arange(sequence_length, dtype=jnp.int32)
    doc_ids = lax.optimization_barrier(jnp.sum((places[:, None] >= ends_at[None, :]).astype(jnp.int32), axis=1))
    matches = doc_ids[:, None] == jnp.arange(doc_lengths.shape[0], dtype=jnp.int32)[None, :]
    begins = lax.optimization_barrier(jnp.sum(jnp.where(matches, starts_at[None, :], 0), axis=1))
    return (doc_ids, places - begins)

def attend(query_block, query_docs, query_places, keys_all, values_all, doc_ids, places):
    raw_scores = jnp.einsum('qhd,khd->hqk', query_block, keys_all, precision=HIGHEST) / math.sqrt(HEAD_SIZE)
    allowed = (doc_ids[None, :] == query_docs[:, None]) & (places[None, :] <= query_places[:, None]) & (query_places[:, None] - places[None, :] < WINDOW)
    scores = low_back(jnp.where(allowed[None], raw_scores, MASKED))
    totals = jax.nn.logsumexp(scores, axis=-1, keepdims=True)
    softmax_out = low(jnp.exp(scores - totals))
    return jnp.einsum('hqk,khd->qhd', softmax_out, values_all, precision=HIGHEST)

def attention_part(resid_in, doc_lengths, input_gain, query_weight, key_value_weight, query_gain, key_gain, out_weight):
    sequence_length = resid_in.shape[0]
    doc_ids, positions = doc_layout(doc_lengths, sequence_length)
    normed = low(rms_norm(resid_in, input_gain))
    query_pre = low_back(product(normed, query_weight)).reshape(sequence_length, QUERY_HEADS, HEAD_SIZE)
    key_value_projected = low_back(product(normed, key_value_weight))
    key_unrotated = key_value_projected[:, :KEY_VALUE_HEADS * HEAD_SIZE].reshape(sequence_length, KEY_VALUE_HEADS, HEAD_SIZE)
    value_rows = low(key_value_projected[:, KEY_VALUE_HEADS * HEAD_SIZE:]).reshape(sequence_length, KEY_VALUE_HEADS, HEAD_SIZE)
    cosine, sine_table = rope_tables(positions.astype(jnp.float32), HEAD_SIZE)
    queries = low(rotate(rms_norm(query_pre, query_gain), cosine, sine_table))
    keys = low(rotate(rms_norm(key_unrotated, key_gain), cosine, sine_table))
    heads_per_group = QUERY_HEADS // KEY_VALUE_HEADS
    keys_all = jnp.repeat(keys, heads_per_group, axis=1)
    values_all = jnp.repeat(value_rows, heads_per_group, axis=1)
    block_rows = min(512, sequence_length)
    block_count = sequence_length // block_rows
    places = jnp.arange(sequence_length, dtype=jnp.int32)

    def one_block(block_items):
        return attend(block_items[0], block_items[1], block_items[2], keys_all, values_all, doc_ids, places)
    attn_rows = lax.map(jax.checkpoint(one_block), (queries.reshape(block_count, block_rows, QUERY_HEADS, HEAD_SIZE), doc_ids.reshape(block_count, block_rows), places.reshape(block_count, block_rows)))
    attended = low(low_back(attn_rows.reshape(sequence_length, QUERY_HEADS * HEAD_SIZE)))
    group_heads = QUERY_HEADS // N_MP
    head_parts = jnp.einsum('tgc,gcd->gtd', attended.reshape(sequence_length, N_MP, group_heads * HEAD_SIZE), out_weight.reshape(N_MP, group_heads * HEAD_SIZE, MODEL_DIM), precision=HIGHEST)
    return resid_in + lax.optimization_barrier(jnp.sum(low(low_back(head_parts)), axis=0))

def expert_block(inputs_all, weights_flat, row_index, pick_index, valid_slot, gate_one, up_one, down_one):
    inputs = low_back(inputs_all[row_index])
    gate_pre = low_back(product(inputs, gate_one))
    up_pre = low_back(product(inputs, up_one))
    hidden = low(jax.nn.silu(gate_pre) * up_pre)
    expert_out = low(low_back(product(hidden, down_one)))
    scale_by = jnp.where(valid_slot, weights_flat[pick_index], 0.0)
    return scale_by[:, None] * expert_out

def moe_part(normed, gate_values, routes, gate_weight, up_weight, down_weight):
    count_rows = normed.shape[0]
    top_count = routes.shape[1]
    flat_routes = routes.reshape(-1)
    sorted_picks = jnp.argsort(flat_routes, stable=True).astype(jnp.int32)
    expert_loads = jnp.bincount(flat_routes, length=EXPERTS).astype(jnp.int32)
    firsts = (jnp.cumsum(expert_loads) - expert_loads).astype(jnp.int32)
    room_size = N_DP * N_MP * CAP
    inputs_all = jnp.concatenate([normed, jnp.zeros((1, MODEL_DIM), jnp.float32)], axis=0)
    weights_flat = gate_values.reshape(-1)
    offsets = jnp.arange(room_size, dtype=jnp.int32)
    checked = jax.checkpoint(expert_block)

    def one_expert(moe_total, scan_items):
        expert, gate_one, up_one, down_one = scan_items
        valid_slot = offsets < expert_loads[expert]
        pick_index = sorted_picks[jnp.minimum(firsts[expert] + offsets, flat_routes.shape[0] - 1)]
        row_index = jnp.where(valid_slot, pick_index // top_count, count_rows)
        expert_term = checked(inputs_all, weights_flat, row_index, pick_index, valid_slot, gate_one, up_one, down_one)
        return (moe_total.at[row_index].add(expert_term), None)
    moe_total, unused = lax.scan(one_expert, jnp.zeros((count_rows + 1, MODEL_DIM), jnp.float32), (jnp.arange(EXPERTS, dtype=jnp.int32), gate_weight, up_weight, down_weight))
    return moe_total[:count_rows]

def forward(tokens_in, input_gain, query_weight, key_value_weight, query_gain, key_gain, out_weight, moe_gain, gate_weight, up_weight, down_weight, gate_values, routes, lengths):
    sequences = lengths.shape[0]
    sequence_length = tokens_in.shape[0] // sequences

    def one_sequence(carried, scan_items):
        return (carried, attention_part(scan_items[0], scan_items[1], input_gain, query_weight, key_value_weight, query_gain, key_gain, out_weight))
    carried, resid = lax.scan(jax.checkpoint(one_sequence), jnp.zeros((), jnp.float32), (tokens_in.reshape(sequences, sequence_length, MODEL_DIM), lengths))
    resid = resid.reshape(sequences * sequence_length, MODEL_DIM)
    normed = low(rms_norm(resid, moe_gain))
    return resid + moe_part(normed, gate_values, routes, gate_weight, up_weight, down_weight)

def reference(tokens, input_gain, query_weight, key_value_weight, query_gain, key_gain, out_weight, moe_gain, gate_weight, up_weight, down_weight, gate_values, routes, lengths, cotangent):
    primals = (tokens.astype(jnp.float32), input_gain, query_weight.astype(jnp.float32), key_value_weight.astype(jnp.float32), query_gain, key_gain, out_weight.astype(jnp.float32), moe_gain, gate_weight.astype(jnp.float32), up_weight.astype(jnp.float32), down_weight.astype(jnp.float32), gate_values)

    def closed(*inputs):
        return forward(*inputs, routes, lengths)
    result, pullback = jax.vjp(closed, *primals)
    gradients = pullback(cotangent.astype(jnp.float32))
    return (result.astype(jnp.bfloat16), gradients[0], gradients[1], gradients[2], gradients[3], gradients[4], gradients[5], gradients[6], gradients[7], gradients[8], gradients[9], gradients[10], gradients[11])
```

```python
import functools
import math

import jax
import jax.numpy as jnp
from jax import lax
from jax.experimental import pallas as pl
from jax.experimental.pallas import tpu as pltpu
from jax.sharding import PartitionSpec as P

WINDOW = 1024
EPSILON = 1e-06
ROPE_BASE = 1000000.0
FAR = 16384.0
VMEM = 56 * 1024 * 1024
LOW = jnp.bfloat16
FULL = jnp.float32


def rms_norm(value_rows, gain_vector):
    return (
        value_rows
        * lax.rsqrt(jnp.mean(value_rows * value_rows, axis=-1, keepdims=True) + EPSILON)
        * gain_vector
    )


def rope_tables(positions, head_width):
    half_width = head_width // 2
    frequency = jnp.exp(
        jnp.arange(half_width, dtype=FULL) * (-2.0 * math.log(ROPE_BASE) / head_width)
    )
    angles = positions[:, None] * frequency[None, :]
    cosine = jnp.cos(angles)
    sine = jnp.sin(angles)
    return (
        jnp.concatenate([cosine, cosine], axis=-1),
        jnp.concatenate([-sine, sine], axis=-1),
    )


def doc_layout(doc_lengths, sequence_length):
    ends_at = jnp.cumsum(doc_lengths)
    starts_at = ends_at - doc_lengths
    places = jnp.arange(sequence_length, dtype=jnp.int32)
    doc_ids = jnp.sum((places[:, None] >= ends_at[None, :]).astype(jnp.int32), axis=1)
    matches = doc_ids[:, None] == jnp.arange(doc_lengths.shape[0], dtype=jnp.int32)[None, :]
    begins = jnp.sum(jnp.where(matches, starts_at[None, :], 0), axis=1)
    return (doc_ids, places - begins)


def matmul(left, right):
    return jnp.dot(left, right, preferred_element_type=FULL)


def contract_last(left, right):
    return lax.dot_general(left, right, (((1,), (1,)), ((), ())), preferred_element_type=FULL)


def contract_first(left, right):
    return lax.dot_general(left, right, (((0,), (0,)), ((), ())), preferred_element_type=FULL)


def ring_shift(shard, axis="mp"):
    length = lax.axis_size(axis)
    return lax.ppermute(shard, axis, [(i, (i + 1) % length) for i in range(length)])


def swap(shard, axis, bit):
    length = lax.axis_size(axis)
    return lax.ppermute(shard, axis, [(i, i ^ bit) for i in range(length)])


def split_rows(rows, count):
    size = rows.shape[0] // count
    return [rows[k * size : (k + 1) * size] for k in range(count)]


def joined_rows(pieces):
    return pieces[0] if len(pieces) == 1 else jnp.concatenate(pieces, axis=0)


def exchange(rows, order):
    pieces = [rows]
    for bit in order:
        half = pieces[0].shape[0] // 2
        came = swap(joined_rows([p[half:] for p in pieces]), "dp", bit)
        pieces = [p[:half] for p in pieces] + split_rows(came, len(pieces))
    return joined_rows(pieces)


def give_back(rows, order):
    pieces = split_rows(rows, 1 << len(order))
    for bit in reversed(order):
        count = len(pieces) // 2
        came = split_rows(swap(joined_rows(pieces[count:]), "dp", bit), count)
        pieces = [joined_rows([k, c]) for k, c in zip(pieces[:count], came)]
    return pieces[0]


def by_place(table, me, order):
    count = len(order)
    rest = table.shape[1:]
    table = table.reshape((2,) * count + rest)
    for axis in range(count):
        turned = (me >> (count - 1 - axis)) & 1
        table = jnp.where(turned == 1, jnp.flip(table, axis), table)
    axes = [count - 1 - (bit.bit_length() - 1) for bit in order]
    axes += list(range(count, count + len(rest)))
    return table.transpose(axes).reshape((1 << count,) + rest)


def by_index(table, me, order):
    count = len(order)
    rest = table.shape[1:]
    table = table.reshape((2,) * count + rest)
    axes = [count - 1 - (bit.bit_length() - 1) for bit in order]
    back = [axes.index(k) for k in range(count)] + list(range(count, count + len(rest)))
    table = table.transpose(back)
    for axis in range(count):
        turned = (me >> (count - 1 - axis)) & 1
        table = jnp.where(turned == 1, jnp.flip(table, axis), table)
    return table.reshape((1 << count,) + rest)


def sum_scatter_rows(rows, order):
    me = lax.axis_index("dp")
    count = len(order)
    size = rows.shape[0] >> count
    parts = rows.reshape((2,) * count + (size, rows.shape[1]))
    axis_of = {bit: count - bit.bit_length() for bit in order}
    left = sorted(order, reverse=True)
    for bit in order:
        axis = left.index(bit)
        side = (me // bit) % 2
        own = lax.dynamic_index_in_dim(parts, side, axis, keepdims=False)
        other = lax.dynamic_index_in_dim(parts, 1 - side, axis, keepdims=False)
        parts = (own.astype(FULL) + swap(other, "dp", bit).astype(FULL)).astype(LOW)
        left.remove(bit)
    return parts


def ring_sum(parts):
    total = None
    for b in list(range(1, len(parts))) + [0]:
        if total is None:
            total = parts[b]
        else:
            total = parts[b] + ring_shift(total.astype(LOW)).astype(FULL)
    return total


def ring_blocks(shard, count):
    blocks = [shard]
    for _ in range(1, count):
        blocks.append(ring_shift(blocks[-1]))
    return blocks


def turned(values):
    return pltpu.roll(values, values.shape[1] // 2, axis=1)


def prep_kernel(at_ref, query_ref, kv_ref, cos_ref, sin_ref, qg_ref, kg_ref, out_ref, kvo_ref):
    width = cos_ref.shape[1]
    cosine, sine = cos_ref[...], sin_ref[...]

    def one(pre, gain):
        rate = lax.rsqrt(jnp.mean(pre * pre, axis=1, keepdims=True) + EPSILON)
        normed = pre * rate * gain
        return (normed * cosine + turned(normed) * sine).astype(LOW)

    for h in range(query_ref.shape[1] // width):
        cols = slice(h * width, (h + 1) * width)
        out_ref[:, cols] = one(query_ref[:, cols], qg_ref[...])
    kvo_ref[:, :width] = one(kv_ref[:, :width], kg_ref[...])
    kvo_ref[:, width:] = kv_ref[:, width:].astype(LOW)


def prepare(at, query_pre, kv_pre, cosine, sine, query_gain, key_gain):
    rows, wide = query_pre.shape
    width = cosine.shape[1]
    step = min(128, rows)
    count = rows // step
    own = lambda i, at: (i, 0)
    table = pl.BlockSpec((step, width), lambda i, at: (at[0] * count + i, 0))
    gain = pl.BlockSpec((1, width), lambda i, at: (0, 0))
    return pl.pallas_call(
        prep_kernel,
        out_shape=(
            jax.ShapeDtypeStruct((rows, wide), LOW),
            jax.ShapeDtypeStruct((rows, 2 * width), LOW),
        ),
        grid_spec=pltpu.PrefetchScalarGridSpec(
            num_scalar_prefetch=1,
            grid=(count,),
            in_specs=[
                pl.BlockSpec((step, wide), own),
                pl.BlockSpec((step, 2 * width), own),
                table,
                table,
                gain,
                gain,
            ],
            out_specs=[pl.BlockSpec((step, wide), own), pl.BlockSpec((step, 2 * width), own)],
        ),
        compiler_params=pltpu.CompilerParams(vmem_limit_bytes=VMEM),
        cost_estimate=pl.CostEstimate(
            flops=rows * wide * 10, bytes_accessed=rows * wide * 8, transcendentals=rows * 16
        ),
    )(at, query_pre, kv_pre, cosine, sine, query_gain, key_gain)


def thirds(values):
    first = values.astype(LOW)
    rest = values - first.astype(FULL)
    second = rest.astype(LOW)
    return first, second, (rest - second.astype(FULL)).astype(LOW)


def attend_kernel(score_scale, docs, at_ref, q_ref, qa_ref, kx_ref, vx_ref, out_ref, aug_ref):
    rows, width = q_ref.shape
    window = WINDOW
    start = pl.multiple_of(at_ref[0] * rows, rows)
    rate = score_scale * math.log2(math.e)
    far = pl.ds(start, rows)
    mid = pl.ds(pl.multiple_of(start + rows, rows), window - rows)
    near = pl.ds(pl.multiple_of(start + window, rows), rows)
    query = jnp.concatenate([q_ref[...], qa_ref[...]], axis=1)
    key_at = lax.broadcasted_iota(jnp.int32, (rows, rows), 1)
    row_at = lax.broadcasted_iota(jnp.int32, (rows, rows), 0)
    upper = key_at > row_at
    corner = jnp.where(
        upper, contract_last(query, kx_ref[far, :]), contract_last(query, kx_ref[near, :])
    )
    corner = jnp.exp2(corner * rate)
    total = matmul(jnp.where(upper, corner, 0.0).astype(LOW), vx_ref[far, :])
    total += matmul(jnp.where(upper, 0.0, corner).astype(LOW), vx_ref[near, :])
    inner = jnp.exp2(contract_last(query, kx_ref[mid, :]) * rate).astype(LOW)
    total += matmul(inner, vx_ref[mid, :])
    sums = total[:, width:]
    out_ref[...] = (total[:, :width] / sums).astype(LOW)
    first, second, third = thirds(jnp.log(sums) * (-1.0 / score_scale))
    lane = lax.broadcasted_iota(jnp.int32, (rows, width), 1)
    aug = qa_ref[...].astype(FULL)
    aug = jnp.where(lane == docs + 1, first.astype(FULL), aug)
    aug = jnp.where(lane == docs + 2, second.astype(FULL), aug)
    aug = jnp.where(lane == docs + 3, third.astype(FULL), aug)
    aug_ref[...] = aug.astype(LOW)


def attend(at, queries, query_aug, keys_wide, values_wide, score_scale, docs):
    rows, wide = queries.shape
    width = query_aug.shape[1]
    heads = wide // width
    head = pl.BlockSpec((rows, width), lambda h, at: (0, h))
    fixed = lambda array: pl.BlockSpec(array.shape, lambda h, at: (0, 0))
    table = pl.BlockSpec((rows, width), lambda h, at: (at[0], 0))
    return pl.pallas_call(
        functools.partial(attend_kernel, score_scale, docs),
        out_shape=(jax.ShapeDtypeStruct((rows, wide), LOW), jax.ShapeDtypeStruct((rows, wide), LOW)),
        grid_spec=pltpu.PrefetchScalarGridSpec(
            num_scalar_prefetch=1,
            grid=(heads,),
            in_specs=[head, table, fixed(keys_wide), fixed(values_wide)],
            out_specs=[head, head],
        ),
        compiler_params=pltpu.CompilerParams(vmem_limit_bytes=VMEM),
        cost_estimate=pl.CostEstimate(
            flops=heads * rows * (WINDOW + rows) * 1024,
            bytes_accessed=rows * wide * 8 + keys_wide.size * 4,
            transcendentals=heads * rows * WINDOW,
        ),
    )(at, queries, query_aug, keys_wide, values_wide)


def attend_back_kernel(
    score_scale,
    at_ref,
    q_ref,
    qa_ref,
    grad_ref,
    out_ref,
    pre_ref,
    cos_ref,
    sin_ref,
    gain_ref,
    kx_ref,
    vx_ref,
    kt_ref,
    low_ref,
    kv_ref,
    gain_grad_ref,
):
    rows, width = q_ref.shape
    window = WINDOW
    start = pl.multiple_of(at_ref[0] * rows, rows)
    rate = score_scale * math.log2(math.e)

    @pl.when(pl.program_id(0) == 0)
    def _():
        kv_ref[...] = jnp.zeros_like(kv_ref)
        gain_grad_ref[...] = jnp.zeros_like(gain_grad_ref)

    query = q_ref[...]
    grad = grad_ref[...]
    query_wide = jnp.concatenate([query, qa_ref[...]], axis=1)
    dots = jnp.sum(grad.astype(FULL) * out_ref[...].astype(FULL), axis=1, keepdims=True)
    first, second, third = thirds(jnp.broadcast_to(-dots, (rows, width)))
    lane = lax.broadcasted_iota(jnp.int32, (rows, width), 1)
    aug = jnp.where(lane == 0, first.astype(FULL), 0.0)
    aug = jnp.where(lane == 1, second.astype(FULL), aug)
    aug = jnp.where(lane == 2, third.astype(FULL), aug)
    grad_wide = jnp.concatenate([grad, aug.astype(LOW)], axis=1)

    def add(part, soft, scores):
        kv_ref[part, :width] += matmul(scores, query)
        kv_ref[part, width:] += matmul(soft, grad)

    mid_size = window - rows
    mid = pl.ds(pl.multiple_of(start + rows, rows), mid_size)
    soft = jnp.exp2(contract_last(kx_ref[mid, :], query_wide) * rate)
    scores = (soft * contract_last(vx_ref[mid, :], grad_wide)).astype(LOW)
    add(slice(rows, rows + mid_size), soft.astype(LOW), scores)
    query_grad = matmul(kt_ref[:, mid], scores)

    far = pl.ds(start, rows)
    near = pl.ds(pl.multiple_of(start + window, rows), rows)
    key_at = lax.broadcasted_iota(jnp.int32, (rows, rows), 0)
    row_at = lax.broadcasted_iota(jnp.int32, (rows, rows), 1)
    upper = key_at > row_at
    corner = jnp.where(
        upper,
        contract_last(kx_ref[far, :], query_wide),
        contract_last(kx_ref[near, :], query_wide),
    )
    soft = jnp.exp2(corner * rate)
    slopes = jnp.where(
        upper, contract_last(vx_ref[far, :], grad_wide), contract_last(vx_ref[near, :], grad_wide)
    )
    scores = soft * slopes
    scores_far = jnp.where(upper, scores, 0.0).astype(LOW)
    scores_near = jnp.where(upper, 0.0, scores).astype(LOW)
    add(slice(0, rows), jnp.where(upper, soft, 0.0).astype(LOW), scores_far)
    add(slice(window, window + rows), jnp.where(upper, 0.0, soft).astype(LOW), scores_near)
    query_grad += matmul(kt_ref[:, far], scores_far)
    query_grad += matmul(kt_ref[:, near], scores_near)

    spread = query_grad.T * score_scale
    spread = spread * cos_ref[...] - sin_ref[...] * turned(spread)
    pre = pre_ref[...]
    pace = lax.rsqrt(jnp.mean(pre * pre, axis=1, keepdims=True) + EPSILON)
    normed = pre * pace
    gain_grad_ref[...] += jnp.sum(spread * normed, axis=0, keepdims=True)
    spread = spread * gain_ref[...]
    low_ref[...] = (
        pace * (spread - normed * jnp.mean(spread * normed, axis=1, keepdims=True))
    ).astype(LOW)


def attend_back(
    at, queries, query_aug, grads, outs, pre, cosine, sine, gain, keys_wide, values_wide, keys_turned, score_scale
):
    rows, wide = queries.shape
    width = cosine.shape[1]
    heads = wide // width
    span = WINDOW + rows
    head = pl.BlockSpec((rows, width), lambda h, at: (0, h))
    fixed = lambda shape: pl.BlockSpec(shape, lambda h, at: (0, 0))
    table = pl.BlockSpec((rows, width), lambda h, at: (at[0], 0))
    return pl.pallas_call(
        functools.partial(attend_back_kernel, score_scale),
        out_shape=(
            jax.ShapeDtypeStruct((rows, wide), LOW),
            jax.ShapeDtypeStruct((span, 2 * width), FULL),
            jax.ShapeDtypeStruct((1, width), FULL),
        ),
        grid_spec=pltpu.PrefetchScalarGridSpec(
            num_scalar_prefetch=1,
            grid=(heads,),
            in_specs=[
                head,
                head,
                head,
                head,
                head,
                table,
                table,
                fixed((1, width)),
                fixed(keys_wide.shape),
                fixed(values_wide.shape),
                fixed(keys_turned.shape),
            ],
            out_specs=[head, fixed((span, 2 * width)), fixed((1, width))],
        ),
        compiler_params=pltpu.CompilerParams(vmem_limit_bytes=VMEM),
        cost_estimate=pl.CostEstimate(
            flops=heads * rows * span * 2048,
            bytes_accessed=rows * wide * 16 + keys_wide.size * 8,
            transcendentals=heads * rows * WINDOW,
        ),
    )(at, queries, query_aug, grads, outs, pre, cosine, sine, gain, keys_wide, values_wide, keys_turned)


def on_device(
    tokens,
    input_gain,
    query_weight,
    key_value_weight,
    query_gain,
    key_gain,
    out_weight,
    moe_gain,
    gate_weight,
    up_weight,
    down_weight,
    gate_values,
    routes,
    lengths,
    cotangent,
):
    row_count, model_width = tokens.shape
    head_width = query_gain.shape[0]
    kv_width = key_value_weight.shape[1] // 2
    local_width = query_weight.shape[1]
    local_heads = local_width // head_width
    mp_count = lax.axis_size("mp")
    dp_count = lax.axis_size("dp")
    expert_count = mp_count * dp_count
    heads_per_group = local_heads * mp_count * head_width // kv_width
    kv_offsets = [m * local_heads // heads_per_group * head_width for m in range(mp_count)]
    mp_place = lax.axis_index("mp")
    dp_place = lax.axis_index("dp")
    kv_offset = mp_place * local_heads // heads_per_group * head_width
    sequence_length = row_count * mp_count
    docs = lengths.shape[1]
    score_scale = 1.0 / math.sqrt(head_width)
    half_index = dp_place % 2
    seq_index = dp_place // 2
    shard_rows = query_weight.shape[0]
    blocks = range(mp_count)
    places = [(mp_place - b) % mp_count for b in blocks]
    spots = [p.reshape((1,)).astype(jnp.int32) for p in places]

    resid_in = tokens.astype(FULL)
    normed_one, norm_one_back = jax.vjp(rms_norm, resid_in, input_gain)
    sequence = ring_blocks(normed_one.astype(LOW), mp_count)
    wq_whole = lax.all_gather(query_weight, "dp", axis=0, tiled=True)
    kv_own = lax.all_gather(
        jnp.concatenate(
            [
                lax.dynamic_slice_in_dim(key_value_weight, kv_offset, head_width, 1),
                lax.dynamic_slice_in_dim(key_value_weight, kv_width + kv_offset, head_width, 1),
            ],
            axis=1,
        ),
        "dp",
        axis=0,
        tiled=True,
    )
    wo_whole = lax.all_gather(out_weight, "dp", axis=1, tiled=True)
    wkv_whole = lax.all_gather(key_value_weight, "dp", axis=0, tiled=True)

    top_count = routes.shape[1]
    routed_mean = row_count * top_count // expert_count
    capacity = max(2, routed_mean + routed_mean // 16)
    capacity = -(-capacity // 8) * 8
    bits = [1 << k for k in range(dp_count.bit_length() - 1)]
    if capacity >= 32:
        cut = (capacity // 2 + 7) // 8 * 8
        streams = [(0, cut, bits[1:] + bits[:1]), (cut, capacity, bits[1:][::-1] + bits[:1])]
    else:
        streams = [(0, capacity, bits[1:] + bits[:1])]
    routes_turned = routes.T
    gates_turned = gate_values.T
    expert_ids = lax.broadcasted_iota(jnp.int32, (expert_count, row_count), 0)
    picked = [routes_turned[k][None, :] == expert_ids for k in range(top_count)]
    member = sum(p.astype(FULL) for p in picked)
    gate_of = sum(jnp.where(picked[k], gates_turned[k][None, :], 0.0) for k in range(top_count))
    ahead = (
        lax.broadcasted_iota(jnp.int32, (row_count, row_count), 0)
        < lax.broadcasted_iota(jnp.int32, (row_count, row_count), 1)
    ).astype(LOW)
    counts = jnp.where(member > 0, matmul(member.astype(LOW), ahead), -1.0)
    plane_counts = lax.all_to_all(
        counts.astype(LOW).reshape(dp_count, mp_count, row_count).transpose(1, 0, 2),
        "mp",
        split_axis=0,
        concat_axis=0,
        tiled=True,
    )
    expert_view = lax.all_to_all(
        jnp.stack([counts, gate_of], axis=1), ("dp", "mp"), split_axis=0, concat_axis=0, tiled=True
    ).reshape(dp_count, mp_count, 2, row_count)

    def slots(table, low, high):
        at = lax.broadcasted_iota(jnp.int32, (1, high - low, 1), 1) + low
        return table[:, None, :] == at.astype(FULL)

    sends = []
    seen = []
    row_gates = []
    for b in blocks:
        here = lax.dynamic_index_in_dim(plane_counts, places[b], 0, keepdims=False).astype(FULL)
        there = lax.dynamic_index_in_dim(expert_view, places[b], 1, keepdims=False)
        picks, finds, weights = [], [], []
        for low, high, order in streams:
            hot = slots(by_place(here, dp_place, order), low, high)
            picks.append(hot.astype(LOW).reshape(dp_count * (high - low), row_count))
            turned_view = by_place(there, dp_place, order[::-1])
            hot = slots(turned_view[:, 0], low, high)
            finds.append(hot)
            weights.append(
                jnp.sum(jnp.where(hot, turned_view[:, 1][:, None, :], 0.0), axis=2).reshape(-1, 1)
            )
        sends.append(picks)
        seen.append(finds)
        row_gates.append(jnp.concatenate(weights, axis=0))

    def dispatch(block, b):
        arrived = [
            exchange(matmul(pick, block).astype(LOW), order)
            for pick, (_, _, order) in zip(sends[b], streams)
        ]
        return joined_rows(arrived)

    def combine(rows, b):
        ends = [dp_count * (high - low) for low, high, _ in streams]
        came = [
            give_back(rows[(sum(ends[:n])) : sum(ends[: n + 1])], streams[n][2])
            for n in range(len(streams))
        ]
        return contract_first(joined_rows(sends[b]), joined_rows(came))

    seq_lengths = lax.dynamic_index_in_dim(lengths, seq_index, 0, keepdims=False)
    docs_whole, places_whole = doc_layout(seq_lengths, 2 * sequence_length)
    doc_ids = lax.dynamic_slice_in_dim(docs_whole, half_index * sequence_length, sequence_length, 0)
    positions = lax.dynamic_slice_in_dim(
        places_whole, half_index * sequence_length, sequence_length, 0
    )
    prior_docs = jnp.where(half_index == 1, docs_whole[:sequence_length], -1)
    docs_pad = jnp.concatenate([prior_docs, doc_ids])
    cosine, sine = rope_tables(positions.astype(FULL), head_width)
    lane = jnp.arange(head_width, dtype=jnp.int32)[None, :]
    query_aug = jnp.where(lane < docs, doc_ids[:, None] != lane, lane == docs).astype(LOW)
    key_hit = jnp.where(lane == docs, docs_pad[:, None] == -1, docs_pad[:, None] == lane)
    key_aug = jnp.where(
        lane <= docs, jnp.where(key_hit, -FAR, 0.0), jnp.where(lane <= docs + 3, 1.0, 0.0)
    ).astype(LOW)
    query_gain_row = query_gain.reshape(1, head_width)
    key_gain_row = key_gain.reshape(1, head_width)

    query_pre, queries = [], []
    kv_rows = jnp.zeros((sequence_length, 2 * head_width), LOW)
    key_pre = jnp.zeros((sequence_length, head_width), FULL)
    for b in blocks:
        pre_b = matmul(sequence[b], wq_whole)
        kv_b = matmul(sequence[b], kv_own)
        queries_b, kv_low = prepare(
            spots[b], pre_b, kv_b, cosine, sine, query_gain_row, key_gain_row
        )
        query_pre.append(pre_b)
        queries.append(queries_b)
        kv_rows = lax.dynamic_update_slice_in_dim(kv_rows, kv_low, places[b] * row_count, 0)
        key_pre = lax.dynamic_update_slice_in_dim(
            key_pre, kv_b[:, :head_width], places[b] * row_count, 0
        )
    prior = lax.ppermute(kv_rows, "dp", [(i, i + 1) for i in range(0, dp_count, 2)])
    keys_pad = jnp.concatenate([prior[:, :head_width], kv_rows[:, :head_width]], axis=0)
    values_pad = jnp.concatenate([prior[:, head_width:], kv_rows[:, head_width:]], axis=0)
    keys_wide = jnp.concatenate([keys_pad, key_aug], axis=1)
    values_wide = jnp.concatenate([values_pad, jnp.ones_like(values_pad)], axis=1)
    keys_turned = keys_pad.T

    attended, augs, head_parts = [None] * mp_count, [None] * mp_count, [None] * mp_count
    for b in list(range(1, mp_count)) + [0]:
        attended[b], augs[b] = attend(
            spots[b], queries[b], query_aug, keys_wide, values_wide, score_scale, docs
        )
        head_parts[b] = matmul(attended[b], wo_whole)
    resid = resid_in + ring_sum(head_parts)
    normed_two, norm_two_back = jax.vjp(rms_norm, resid, moe_gain)

    gate_one, up_one, down_one = gate_weight[0], up_weight[0], down_weight[0]
    cot_blocks = ring_blocks(cotangent, mp_count)
    normed_blocks = ring_blocks(normed_two.astype(LOW), mp_count)
    inputs, hiddens, scaled, gate_grads, up_grads, outs, gate_rows = [], [], [], [], [], [], []
    resid_parts = []
    cot_rows = [dispatch(cot_blocks[b], b) for b in blocks]
    for b in blocks:
        rows_b = dispatch(normed_blocks[b], b)
        gate_pre = matmul(rows_b, gate_one)
        up_pre = matmul(rows_b, up_one)
        sigmoid_gate = jax.nn.sigmoid(gate_pre)
        silu_gate = gate_pre * sigmoid_gate
        hidden = (silu_gate * up_pre).astype(LOW)
        scaled_b = (row_gates[b] * cot_rows[b].astype(FULL)).astype(LOW)
        grad_hidden = contract_last(scaled_b, down_one)
        gate_grad = (
            grad_hidden * up_pre * sigmoid_gate * (1.0 + gate_pre * (1.0 - sigmoid_gate))
        ).astype(LOW)
        up_grad = (grad_hidden * silu_gate).astype(LOW)
        grad_in = (contract_last(gate_grad, gate_one) + contract_last(up_grad, up_one)).astype(LOW)
        resid_parts.append(combine(grad_in, b))
        inputs.append(rows_b)
        hiddens.append(hidden)
        scaled.append(scaled_b)
        gate_grads.append(gate_grad)
        up_grads.append(up_grad)
    grad_moe_normed = ring_sum(resid_parts)
    grad_resid_norm, moe_gain_part = norm_two_back(grad_moe_normed)
    grad_resid = cotangent.astype(FULL) + grad_resid_norm
    back = ring_blocks(grad_resid.astype(LOW), mp_count)

    out_parts = []
    gate_grad_parts = []
    for b in blocks:
        out_b = matmul(hiddens[b], down_one)
        dots = jnp.sum(out_b * cot_rows[b].astype(FULL), axis=1, keepdims=True)
        out_low = (row_gates[b] * out_b).astype(LOW)
        out_low, _ = lax.optimization_barrier((out_low, grad_moe_normed))
        out_parts.append(combine(out_low, b))
        found = 0.0
        base = 0
        for (low, high, order), hot in zip(streams, seen[b]):
            size = dp_count * (high - low)
            mine = dots[base : base + size].reshape(dp_count, high - low, 1)
            base += size
            found += by_index(jnp.sum(jnp.where(hot, mine, 0.0), axis=1), dp_place, order[::-1])
        gate_grad_parts.append(found)
    block_out = (resid + ring_sum(out_parts)).astype(LOW)
    spread = jnp.stack(
        [
            sum(jnp.where(places[b] == p, gate_grad_parts[b], 0.0) for b in blocks)
            for p in range(mp_count)
        ],
        axis=1,
    ).reshape(expert_count, row_count)
    spread = lax.all_to_all(spread, ("dp", "mp"), split_axis=0, concat_axis=0, tiled=True)
    gate_values_grad = jnp.stack(
        [jnp.sum(jnp.where(picked[k], spread, 0.0), axis=0) for k in range(top_count)], axis=1
    )
    inputs_all = joined_rows(inputs)
    down_weight_grad = contract_first(joined_rows(hiddens), joined_rows(scaled))[None]
    gate_weight_grad = contract_first(inputs_all, joined_rows(gate_grads))[None]
    up_weight_grad = contract_first(inputs_all, joined_rows(up_grads))[None]

    out_weight_grad = lax.psum_scatter(
        contract_first(joined_rows(attended), joined_rows(back)).astype(LOW),
        "dp",
        scatter_dimension=1,
        tiled=True,
    ).astype(FULL)
    kv_grads = jnp.zeros((2 * sequence_length, 2 * head_width), FULL)
    query_low, query_gain_part, input_parts = [], 0.0, []
    for b in blocks:
        grad_attended = contract_last(back[b], wo_whole).astype(LOW)
        low_b, kv_b, gain_b = attend_back(
            spots[b],
            queries[b],
            augs[b],
            grad_attended,
            attended[b],
            query_pre[b],
            cosine,
            sine,
            query_gain_row,
            keys_wide,
            values_wide,
            keys_turned,
            score_scale,
        )
        at = places[b] * row_count
        kv_grads = lax.dynamic_update_slice_in_dim(
            kv_grads, lax.dynamic_slice_in_dim(kv_grads, at, kv_b.shape[0], 0) + kv_b, at, 0
        )
        query_low.append(low_b)
        query_gain_part += gain_b[0]
        input_parts.append(contract_last(low_b, wq_whole))
    returned = lax.ppermute(
        kv_grads[:sequence_length].astype(LOW), "dp", [(i + 1, i) for i in range(0, dp_count, 2)]
    )
    kv_total = kv_grads[sequence_length:] + jnp.where(half_index == 0, returned.astype(FULL), 0.0)

    def key_prep(pre, gain):
        normed = rms_norm(pre, gain)
        return normed * cosine + jnp.roll(normed, head_width // 2, axis=1) * sine

    _, key_back = jax.vjp(key_prep, key_pre, key_gain)
    grad_key_pre, key_gain_part = key_back(kv_total[:, :head_width] * score_scale)
    kv_low = jnp.concatenate([grad_key_pre, kv_total[:, head_width:]], axis=1).astype(LOW)
    kv_spread = lax.all_to_all(
        kv_low.reshape(mp_count, row_count, 2 * head_width),
        "mp",
        split_axis=0,
        concat_axis=0,
        tiled=True,
    )
    grad_normed_one = ring_sum(input_parts)
    for m in blocks:
        cols = kv_offsets[m]
        grad_normed_one += contract_last(
            kv_spread[m, :, :head_width], wkv_whole[:, cols : cols + head_width]
        )
        cols += kv_width
        grad_normed_one += contract_last(
            kv_spread[m, :, head_width:], wkv_whole[:, cols : cols + head_width]
        )
    grad_in_norm, input_gain_part = norm_one_back(grad_normed_one)
    tokens_grad = grad_resid + grad_in_norm

    kv_blocks = [
        lax.dynamic_slice_in_dim(kv_low, places[b] * row_count, row_count, 0) for b in blocks
    ]
    joined = jnp.concatenate([joined_rows(query_low), joined_rows(kv_blocks)], axis=1)
    weight_part = contract_first(joined_rows(sequence), joined).astype(LOW)
    half = (weight_part.shape[1] // 256) * 128
    summed_rows = jnp.concatenate(
        [
            sum_scatter_rows(weight_part[:, :half], bits),
            sum_scatter_rows(weight_part[:, half:], bits[:1] + bits[1:][::-1]),
        ],
        axis=1,
    )
    query_weight_grad = summed_rows[:, :local_width].astype(FULL)
    own_cols = lax.all_gather(summed_rows[:, local_width:], "mp", axis=0).astype(FULL)
    kv_parts = [None] * (2 * kv_width // head_width)
    for m in blocks:
        for side in range(2):
            at = (kv_offsets[m] + side * kv_width) // head_width
            term = own_cols[m, :, side * head_width : (side + 1) * head_width]
            kv_parts[at] = term if kv_parts[at] is None else kv_parts[at] + term
    kv_weight_grad = jnp.concatenate(kv_parts, axis=1)

    gains = jnp.concatenate([moe_gain_part, query_gain_part, key_gain_part, input_gain_part])
    for bit in bits:
        gains += swap(gains, "dp", bit)
    step = 1
    while step < mp_count:
        gains += swap(gains, "mp", step)
        step *= 2
    ends = [model_width, model_width + head_width, model_width + 2 * head_width]
    return (
        block_out,
        tokens_grad,
        gains[ends[2] :],
        query_weight_grad,
        kv_weight_grad,
        gains[ends[0] : ends[1]],
        gains[ends[1] : ends[2]],
        out_weight_grad,
        gains[: ends[0]],
        gate_weight_grad,
        up_weight_grad,
        down_weight_grad,
        gate_values_grad,
    )


def solution(mesh):
    both = ("dp", "mp")
    rows = P(both, None)
    experts = P(both, None, None)
    return jax.shard_map(
        on_device,
        mesh=mesh,
        in_specs=(
            rows,
            P(),
            P("dp", "mp"),
            P("dp", None),
            P(),
            P(),
            P("mp", "dp"),
            P(),
            experts,
            experts,
            experts,
            rows,
            rows,
            P(),
            rows,
        ),
        out_specs=(
            rows,
            rows,
            P(),
            P("dp", "mp"),
            P("dp", None),
            P(),
            P(),
            P("mp", "dp"),
            P(),
            experts,
            experts,
            experts,
            rows,
        ),
        check_vma=False,
    )
```

```python
import functools
import math

import jax
import jax.numpy as jnp
from jax import lax
from jax.experimental import pallas as pl
from jax.experimental.pallas import tpu as pltpu
from jax.sharding import PartitionSpec as P

WINDOW = 1024
EPSILON = 1e-06
ROPE_BASE = 1000000.0
FAR = 16384.0
VMEM = 56 * 1024 * 1024
LOW = jnp.bfloat16
FULL = jnp.float32


def rms_norm(value_rows, gain_vector):
    return (
        value_rows
        * lax.rsqrt(jnp.mean(value_rows * value_rows, axis=-1, keepdims=True) + EPSILON)
        * gain_vector
    )


def rope_tables(positions, head_width):
    half_width = head_width // 2
    frequency = jnp.exp(
        jnp.arange(half_width, dtype=FULL) * (-2.0 * math.log(ROPE_BASE) / head_width)
    )
    angles = positions[:, None] * frequency[None, :]
    cosine = jnp.cos(angles)
    sine = jnp.sin(angles)
    return (
        jnp.concatenate([cosine, cosine], axis=-1),
        jnp.concatenate([-sine, sine], axis=-1),
    )


def doc_layout(doc_lengths, sequence_length):
    ends_at = jnp.cumsum(doc_lengths)
    starts_at = ends_at - doc_lengths
    places = jnp.arange(sequence_length, dtype=jnp.int32)
    doc_ids = jnp.sum((places[:, None] >= ends_at[None, :]).astype(jnp.int32), axis=1)
    matches = doc_ids[:, None] == jnp.arange(doc_lengths.shape[0], dtype=jnp.int32)[None, :]
    begins = jnp.sum(jnp.where(matches, starts_at[None, :], 0), axis=1)
    return (doc_ids, places - begins)


def matmul(left, right):
    return jnp.dot(left, right, preferred_element_type=FULL)


def contract_last(left, right):
    return lax.dot_general(left, right, (((1,), (1,)), ((), ())), preferred_element_type=FULL)


def contract_first(left, right):
    return lax.dot_general(left, right, (((0,), (0,)), ((), ())), preferred_element_type=FULL)


def ring_shift(shard, axis="mp"):
    length = lax.axis_size(axis)
    return lax.ppermute(shard, axis, [(i, (i + 1) % length) for i in range(length)])


def swap(shard, axis, bit):
    length = lax.axis_size(axis)
    return lax.ppermute(shard, axis, [(i, i ^ bit) for i in range(length)])


def joined_rows(pieces):
    return pieces[0] if len(pieces) == 1 else jnp.concatenate(pieces, axis=0)


def nought(array):
    return jnp.minimum(jnp.abs(array[(0,) * array.ndim].astype(FULL)), 0.0)


def behind(array, *others):
    return (array.astype(FULL) + sum(nought(o) for o in others)).astype(array.dtype)


def sum_scatter_rows(rows, order):
    me = lax.axis_index("dp")
    count = len(order)
    size = rows.shape[0] >> count
    parts = rows.reshape((2,) * count + (size, rows.shape[1]))
    axis_of = {bit: count - bit.bit_length() for bit in order}
    left = sorted(order, reverse=True)
    for bit in order:
        axis = left.index(bit)
        side = (me // bit) % 2
        own = lax.dynamic_index_in_dim(parts, side, axis, keepdims=False)
        other = lax.dynamic_index_in_dim(parts, 1 - side, axis, keepdims=False)
        parts = (own.astype(FULL) + swap(other, "dp", bit).astype(FULL)).astype(LOW)
        left.remove(bit)
    return parts


def ring_sum(parts):
    total = None
    for b in list(range(1, len(parts))) + [0]:
        if total is None:
            total = parts[b]
        else:
            total = parts[b] + ring_shift(total.astype(LOW)).astype(FULL)
    return total


def ring_blocks(shard, count):
    blocks = [shard]
    for _ in range(1, count):
        blocks.append(ring_shift(blocks[-1]))
    return blocks


def turned(values):
    return pltpu.roll(values, values.shape[1] // 2, axis=1)


def prep_kernel(at_ref, query_ref, kv_ref, cos_ref, sin_ref, qg_ref, kg_ref, out_ref, kvo_ref):
    width = cos_ref.shape[1]
    cosine, sine = cos_ref[...], sin_ref[...]

    def one(pre, gain):
        rate = lax.rsqrt(jnp.mean(pre * pre, axis=1, keepdims=True) + EPSILON)
        normed = pre * rate * gain
        return (normed * cosine + turned(normed) * sine).astype(LOW)

    for h in range(query_ref.shape[1] // width):
        cols = slice(h * width, (h + 1) * width)
        out_ref[:, cols] = one(query_ref[:, cols], qg_ref[...])
    kvo_ref[:, :width] = one(kv_ref[:, :width], kg_ref[...])
    kvo_ref[:, width:] = kv_ref[:, width:].astype(LOW)


def prepare(at, query_pre, kv_pre, cosine, sine, query_gain, key_gain):
    rows, wide = query_pre.shape
    width = cosine.shape[1]
    step = min(128, rows)
    count = rows // step
    own = lambda i, at: (i, 0)
    table = pl.BlockSpec((step, width), lambda i, at: (at[0] * count + i, 0))
    gain = pl.BlockSpec((1, width), lambda i, at: (0, 0))
    return pl.pallas_call(
        prep_kernel,
        out_shape=(
            jax.ShapeDtypeStruct((rows, wide), LOW),
            jax.ShapeDtypeStruct((rows, 2 * width), LOW),
        ),
        grid_spec=pltpu.PrefetchScalarGridSpec(
            num_scalar_prefetch=1,
            grid=(count,),
            in_specs=[
                pl.BlockSpec((step, wide), own),
                pl.BlockSpec((step, 2 * width), own),
                table,
                table,
                gain,
                gain,
            ],
            out_specs=[pl.BlockSpec((step, wide), own), pl.BlockSpec((step, 2 * width), own)],
        ),
        compiler_params=pltpu.CompilerParams(vmem_limit_bytes=VMEM),
        cost_estimate=pl.CostEstimate(
            flops=rows * wide * 10, bytes_accessed=rows * wide * 8, transcendentals=rows * 16
        ),
    )(at, query_pre, kv_pre, cosine, sine, query_gain, key_gain)


def thirds(values):
    first = values.astype(LOW)
    rest = values - first.astype(FULL)
    second = rest.astype(LOW)
    return first, second, (rest - second.astype(FULL)).astype(LOW)


def attend_kernel(score_scale, docs, at_ref, q_ref, qa_ref, kx_ref, vx_ref, out_ref, aug_ref):
    rows, width = q_ref.shape
    window = WINDOW
    start = pl.multiple_of(at_ref[0] * rows, rows)
    rate = score_scale * math.log2(math.e)
    far = pl.ds(start, rows)
    mid = pl.ds(pl.multiple_of(start + rows, rows), window - rows)
    near = pl.ds(pl.multiple_of(start + window, rows), rows)
    query = jnp.concatenate([q_ref[...], qa_ref[...]], axis=1)
    key_at = lax.broadcasted_iota(jnp.int32, (rows, rows), 1)
    row_at = lax.broadcasted_iota(jnp.int32, (rows, rows), 0)
    upper = key_at > row_at
    corner = jnp.where(
        upper, contract_last(query, kx_ref[far, :]), contract_last(query, kx_ref[near, :])
    )
    corner = jnp.exp2(corner * rate)
    total = matmul(jnp.where(upper, corner, 0.0).astype(LOW), vx_ref[far, :])
    total += matmul(jnp.where(upper, 0.0, corner).astype(LOW), vx_ref[near, :])
    inner = jnp.exp2(contract_last(query, kx_ref[mid, :]) * rate).astype(LOW)
    total += matmul(inner, vx_ref[mid, :])
    sums = total[:, width:]
    out_ref[...] = (total[:, :width] / sums).astype(LOW)
    first, second, third = thirds(jnp.log(sums) * (-1.0 / score_scale))
    lane = lax.broadcasted_iota(jnp.int32, (rows, width), 1)
    aug = qa_ref[...].astype(FULL)
    aug = jnp.where(lane == docs + 1, first.astype(FULL), aug)
    aug = jnp.where(lane == docs + 2, second.astype(FULL), aug)
    aug = jnp.where(lane == docs + 3, third.astype(FULL), aug)
    aug_ref[...] = aug.astype(LOW)


def attend(at, queries, query_aug, keys_wide, values_wide, score_scale, docs):
    rows, wide = queries.shape
    width = query_aug.shape[1]
    heads = wide // width
    head = pl.BlockSpec((rows, width), lambda h, at: (0, h))
    fixed = lambda array: pl.BlockSpec(array.shape, lambda h, at: (0, 0))
    table = pl.BlockSpec((rows, width), lambda h, at: (at[0], 0))
    return pl.pallas_call(
        functools.partial(attend_kernel, score_scale, docs),
        out_shape=(jax.ShapeDtypeStruct((rows, wide), LOW), jax.ShapeDtypeStruct((rows, wide), LOW)),
        grid_spec=pltpu.PrefetchScalarGridSpec(
            num_scalar_prefetch=1,
            grid=(heads,),
            in_specs=[head, table, fixed(keys_wide), fixed(values_wide)],
            out_specs=[head, head],
        ),
        compiler_params=pltpu.CompilerParams(vmem_limit_bytes=VMEM),
        cost_estimate=pl.CostEstimate(
            flops=heads * rows * (WINDOW + rows) * 1024,
            bytes_accessed=rows * wide * 8 + keys_wide.size * 4,
            transcendentals=heads * rows * WINDOW,
        ),
    )(at, queries, query_aug, keys_wide, values_wide)


def attend_back_kernel(
    score_scale,
    at_ref,
    q_ref,
    qa_ref,
    grad_ref,
    out_ref,
    pre_ref,
    cos_ref,
    sin_ref,
    gain_ref,
    kx_ref,
    vx_ref,
    kt_ref,
    low_ref,
    kv_ref,
    gain_grad_ref,
):
    rows, width = q_ref.shape
    window = WINDOW
    start = pl.multiple_of(at_ref[0] * rows, rows)
    rate = score_scale * math.log2(math.e)

    @pl.when(pl.program_id(0) == 0)
    def _():
        kv_ref[...] = jnp.zeros_like(kv_ref)
        gain_grad_ref[...] = jnp.zeros_like(gain_grad_ref)

    query = q_ref[...]
    grad = grad_ref[...]
    query_wide = jnp.concatenate([query, qa_ref[...]], axis=1)
    dots = jnp.sum(grad.astype(FULL) * out_ref[...].astype(FULL), axis=1, keepdims=True)
    first, second, third = thirds(jnp.broadcast_to(-dots, (rows, width)))
    lane = lax.broadcasted_iota(jnp.int32, (rows, width), 1)
    aug = jnp.where(lane == 0, first.astype(FULL), 0.0)
    aug = jnp.where(lane == 1, second.astype(FULL), aug)
    aug = jnp.where(lane == 2, third.astype(FULL), aug)
    grad_wide = jnp.concatenate([grad, aug.astype(LOW)], axis=1)

    def add(part, soft, scores):
        kv_ref[part, :width] += matmul(scores, query)
        kv_ref[part, width:] += matmul(soft, grad)

    mid_size = window - rows
    mid = pl.ds(pl.multiple_of(start + rows, rows), mid_size)
    soft = jnp.exp2(contract_last(kx_ref[mid, :], query_wide) * rate)
    scores = (soft * contract_last(vx_ref[mid, :], grad_wide)).astype(LOW)
    add(slice(rows, rows + mid_size), soft.astype(LOW), scores)
    query_grad = matmul(kt_ref[:, mid], scores)

    far = pl.ds(start, rows)
    near = pl.ds(pl.multiple_of(start + window, rows), rows)
    key_at = lax.broadcasted_iota(jnp.int32, (rows, rows), 0)
    row_at = lax.broadcasted_iota(jnp.int32, (rows, rows), 1)
    upper = key_at > row_at
    corner = jnp.where(
        upper,
        contract_last(kx_ref[far, :], query_wide),
        contract_last(kx_ref[near, :], query_wide),
    )
    soft = jnp.exp2(corner * rate)
    slopes = jnp.where(
        upper, contract_last(vx_ref[far, :], grad_wide), contract_last(vx_ref[near, :], grad_wide)
    )
    scores = soft * slopes
    scores_far = jnp.where(upper, scores, 0.0).astype(LOW)
    scores_near = jnp.where(upper, 0.0, scores).astype(LOW)
    add(slice(0, rows), jnp.where(upper, soft, 0.0).astype(LOW), scores_far)
    add(slice(window, window + rows), jnp.where(upper, 0.0, soft).astype(LOW), scores_near)
    query_grad += matmul(kt_ref[:, far], scores_far)
    query_grad += matmul(kt_ref[:, near], scores_near)

    spread = query_grad.T * score_scale
    spread = spread * cos_ref[...] - sin_ref[...] * turned(spread)
    pre = pre_ref[...]
    pace = lax.rsqrt(jnp.mean(pre * pre, axis=1, keepdims=True) + EPSILON)
    normed = pre * pace
    gain_grad_ref[...] += jnp.sum(spread * normed, axis=0, keepdims=True)
    spread = spread * gain_ref[...]
    low_ref[...] = (
        pace * (spread - normed * jnp.mean(spread * normed, axis=1, keepdims=True))
    ).astype(LOW)


def attend_back(
    at, queries, query_aug, grads, outs, pre, cosine, sine, gain, keys_wide, values_wide, keys_turned, score_scale
):
    rows, wide = queries.shape
    width = cosine.shape[1]
    heads = wide // width
    span = WINDOW + rows
    head = pl.BlockSpec((rows, width), lambda h, at: (0, h))
    fixed = lambda shape: pl.BlockSpec(shape, lambda h, at: (0, 0))
    table = pl.BlockSpec((rows, width), lambda h, at: (at[0], 0))
    return pl.pallas_call(
        functools.partial(attend_back_kernel, score_scale),
        out_shape=(
            jax.ShapeDtypeStruct((rows, wide), LOW),
            jax.ShapeDtypeStruct((span, 2 * width), FULL),
            jax.ShapeDtypeStruct((1, width), FULL),
        ),
        grid_spec=pltpu.PrefetchScalarGridSpec(
            num_scalar_prefetch=1,
            grid=(heads,),
            in_specs=[
                head,
                head,
                head,
                head,
                head,
                table,
                table,
                fixed((1, width)),
                fixed(keys_wide.shape),
                fixed(values_wide.shape),
                fixed(keys_turned.shape),
            ],
            out_specs=[head, fixed((span, 2 * width)), fixed((1, width))],
        ),
        compiler_params=pltpu.CompilerParams(vmem_limit_bytes=VMEM),
        cost_estimate=pl.CostEstimate(
            flops=heads * rows * span * 2048,
            bytes_accessed=rows * wide * 16 + keys_wide.size * 8,
            transcendentals=heads * rows * WINDOW,
        ),
    )(at, queries, query_aug, grads, outs, pre, cosine, sine, gain, keys_wide, values_wide, keys_turned)


def on_device(
    tokens,
    input_gain,
    query_weight,
    key_value_weight,
    query_gain,
    key_gain,
    out_weight,
    moe_gain,
    gate_weight,
    up_weight,
    down_weight,
    gate_values,
    routes,
    lengths,
    cotangent,
):
    row_count, model_width = tokens.shape
    head_width = query_gain.shape[0]
    kv_width = key_value_weight.shape[1] // 2
    local_width = query_weight.shape[1]
    local_heads = local_width // head_width
    mp_count = lax.axis_size("mp")
    dp_count = lax.axis_size("dp")
    expert_count = mp_count * dp_count
    heads_per_group = local_heads * mp_count * head_width // kv_width
    kv_offsets = [m * local_heads // heads_per_group * head_width for m in range(mp_count)]
    mp_place = lax.axis_index("mp")
    dp_place = lax.axis_index("dp")
    kv_offset = mp_place * local_heads // heads_per_group * head_width
    sequence_length = row_count * mp_count
    docs = lengths.shape[1]
    score_scale = 1.0 / math.sqrt(head_width)
    half_index = dp_place % 2
    seq_index = dp_place // 2
    shard_rows = query_weight.shape[0]
    blocks = range(mp_count)
    places = [(mp_place - b) % mp_count for b in blocks]
    spots = [p.reshape((1,)).astype(jnp.int32) for p in places]

    resid_in = tokens.astype(FULL)
    normed_one, norm_one_back = jax.vjp(rms_norm, resid_in, input_gain)
    sequence = ring_blocks(normed_one.astype(LOW), mp_count)
    wq_whole = lax.all_gather(query_weight, "dp", axis=0, tiled=True)
    kv_own = lax.all_gather(
        jnp.concatenate(
            [
                lax.dynamic_slice_in_dim(key_value_weight, kv_offset, head_width, 1),
                lax.dynamic_slice_in_dim(key_value_weight, kv_width + kv_offset, head_width, 1),
            ],
            axis=1,
        ),
        "dp",
        axis=0,
        tiled=True,
    )
    wo_whole = lax.all_gather(out_weight, "dp", axis=1, tiled=True)
    wkv_whole = lax.all_gather(key_value_weight, "dp", axis=0, tiled=True)

    top_count = routes.shape[1]
    routed_mean = row_count * top_count // expert_count
    capacity = max(2, routed_mean + routed_mean // 16)
    group_size = 2
    groups = [list(range(b, b + group_size)) for b in range(0, mp_count, group_size)]
    group_rows = group_size * capacity
    bits = [1 << k for k in range(dp_count.bit_length() - 1)]
    routes_turned = routes.T
    gates_turned = gate_values.T
    expert_ids = lax.broadcasted_iota(jnp.int32, (expert_count, row_count), 0)
    picked = [routes_turned[k][None, :] == expert_ids for k in range(top_count)]
    member = sum(p.astype(FULL) for p in picked)
    gate_of = sum(jnp.where(picked[k], gates_turned[k][None, :], 0.0) for k in range(top_count))
    ahead = (
        lax.broadcasted_iota(jnp.int32, (row_count, row_count), 0)
        < lax.broadcasted_iota(jnp.int32, (row_count, row_count), 1)
    ).astype(LOW)
    counts = jnp.where(member > 0, matmul(member.astype(LOW), ahead), -1.0)
    plane_counts = lax.all_to_all(
        counts.astype(LOW).reshape(dp_count, mp_count, row_count).transpose(1, 0, 2),
        "mp",
        split_axis=0,
        concat_axis=0,
        tiled=True,
    )
    expert_view = lax.all_to_all(
        jnp.stack([counts, gate_of], axis=1), ("dp", "mp"), split_axis=0, concat_axis=0, tiled=True
    ).reshape(dp_count, mp_count, 2, row_count)

    row_ids = lax.broadcasted_iota(jnp.int32, (dp_count * group_rows, dp_count), 0)
    widen = (
        row_ids // group_rows == lax.broadcasted_iota(jnp.int32, row_ids.shape, 1)
    ).astype(LOW)
    row_ids = lax.broadcasted_iota(jnp.int32, (dp_count * group_rows, group_size * row_count), 0)
    token_ids = lax.broadcasted_iota(jnp.int32, row_ids.shape, 1)
    aim = jnp.where(
        row_ids % group_rows // capacity == token_ids // row_count, row_ids % capacity, -5
    ).astype(FULL)

    def hot_rows(table):
        return matmul(widen, table.astype(LOW)) == aim

    sends, seen, row_gates = [], [], []
    for group in groups:
        here = jnp.concatenate(
            [lax.dynamic_index_in_dim(plane_counts, places[b], 0, keepdims=False) for b in group],
            axis=1,
        )
        there = jnp.concatenate(
            [lax.dynamic_index_in_dim(expert_view, places[b], 1, keepdims=False) for b in group],
            axis=2,
        )
        sends.append(hot_rows(here).astype(LOW))
        hot = hot_rows(there[:, 0])
        seen.append(hot)
        spread_gates = jnp.dot(
            widen.astype(FULL), there[:, 1], precision=lax.Precision.HIGHEST
        )
        row_gates.append(jnp.sum(jnp.where(hot, spread_gates, 0.0), axis=1, keepdims=True))

    def plane_turn(rows):
        return lax.all_to_all(
            rows.reshape(dp_count, group_rows, model_width),
            "dp",
            split_axis=0,
            concat_axis=0,
            tiled=True,
        ).reshape(dp_count * group_rows, model_width)

    def dispatch(pieces, g):
        return plane_turn(matmul(sends[g], joined_rows(pieces)).astype(LOW))

    def place(came, g):
        sums = contract_first(sends[g], came)
        return [sums[k * row_count : (k + 1) * row_count] for k in range(group_size)]

    seq_lengths = lax.dynamic_index_in_dim(lengths, seq_index, 0, keepdims=False)
    docs_whole, places_whole = doc_layout(seq_lengths, 2 * sequence_length)
    doc_ids = lax.dynamic_slice_in_dim(docs_whole, half_index * sequence_length, sequence_length, 0)
    positions = lax.dynamic_slice_in_dim(
        places_whole, half_index * sequence_length, sequence_length, 0
    )
    prior_docs = jnp.where(half_index == 1, docs_whole[:sequence_length], -1)
    docs_pad = jnp.concatenate([prior_docs, doc_ids])
    cosine, sine = rope_tables(positions.astype(FULL), head_width)
    lane = jnp.arange(head_width, dtype=jnp.int32)[None, :]
    query_aug = jnp.where(lane < docs, doc_ids[:, None] != lane, lane == docs).astype(LOW)
    key_hit = jnp.where(lane == docs, docs_pad[:, None] == -1, docs_pad[:, None] == lane)
    key_aug = jnp.where(
        lane <= docs, jnp.where(key_hit, -FAR, 0.0), jnp.where(lane <= docs + 3, 1.0, 0.0)
    ).astype(LOW)
    query_gain_row = query_gain.reshape(1, head_width)
    key_gain_row = key_gain.reshape(1, head_width)

    query_pre, queries = [], []
    kv_rows = jnp.zeros((sequence_length, 2 * head_width), LOW)
    key_pre = jnp.zeros((sequence_length, head_width), FULL)
    for b in blocks:
        pre_b = matmul(sequence[b], wq_whole)
        kv_b = matmul(sequence[b], kv_own)
        queries_b, kv_low = prepare(
            spots[b], pre_b, kv_b, cosine, sine, query_gain_row, key_gain_row
        )
        query_pre.append(pre_b)
        queries.append(queries_b)
        kv_rows = lax.dynamic_update_slice_in_dim(kv_rows, kv_low, places[b] * row_count, 0)
        key_pre = lax.dynamic_update_slice_in_dim(
            key_pre, kv_b[:, :head_width], places[b] * row_count, 0
        )
    prior = lax.ppermute(kv_rows, "dp", [(i, i + 1) for i in range(0, dp_count, 2)])
    keys_pad = jnp.concatenate([prior[:, :head_width], kv_rows[:, :head_width]], axis=0)
    values_pad = jnp.concatenate([prior[:, head_width:], kv_rows[:, head_width:]], axis=0)
    keys_wide = jnp.concatenate([keys_pad, key_aug], axis=1)
    values_wide = jnp.concatenate([values_pad, jnp.ones_like(values_pad)], axis=1)
    keys_turned = keys_pad.T

    cot_blocks = [cotangent]
    cot_rows = []

    attended, augs, head_parts = [None] * mp_count, [None] * mp_count, [None] * mp_count
    for b in list(range(1, mp_count)) + [0]:
        attended[b], augs[b] = attend(
            spots[b], queries[b], query_aug, keys_wide, values_wide, score_scale, docs
        )
        head_parts[b] = matmul(attended[b], wo_whole)
        if b > 0:
            waits = sequence[-1] if b == 1 else keys_wide if b == 2 else attended[b - 2]
            cot_blocks.append(ring_shift(behind(cot_blocks[-1], waits)))
    for g, group in enumerate(groups):
        cot_rows.append(dispatch([cot_blocks[b] for b in group], g))
    resid = resid_in + ring_sum(head_parts)
    normed_two, norm_two_back = jax.vjp(rms_norm, resid, moe_gain)

    gate_one, up_one, down_one = gate_weight[0], up_weight[0], down_weight[0]
    normed_blocks = ring_blocks(normed_two.astype(LOW), mp_count)
    inputs, hiddens, scaled, gate_grads, up_grads = [], [], [], [], []
    resid_parts, came = [], None
    for g, group in enumerate(groups):
        rows_g = dispatch([normed_blocks[b] for b in group], g)
        gate_pre = matmul(rows_g, gate_one)
        up_pre = matmul(rows_g, up_one)
        sigmoid_gate = jax.nn.sigmoid(gate_pre)
        silu_gate = gate_pre * sigmoid_gate
        hidden = (silu_gate * up_pre).astype(LOW)
        scaled_g = (row_gates[g] * cot_rows[g].astype(FULL)).astype(LOW)
        grad_hidden = contract_last(scaled_g, down_one)
        gate_grad = (
            grad_hidden * up_pre * sigmoid_gate * (1.0 + gate_pre * (1.0 - sigmoid_gate))
        ).astype(LOW)
        up_grad = (grad_hidden * silu_gate).astype(LOW)
        grad_in = (contract_last(gate_grad, gate_one) + contract_last(up_grad, up_one)).astype(LOW)
        came = plane_turn(grad_in)
        resid_parts += place(came, g)
        inputs.append(rows_g)
        hiddens.append(hidden)
        scaled.append(scaled_g)
        gate_grads.append(gate_grad)
        up_grads.append(up_grad)
    grad_moe_normed = ring_sum(resid_parts)
    grad_resid_norm, moe_gain_part = norm_two_back(grad_moe_normed)
    grad_resid = cotangent.astype(FULL) + grad_resid_norm
    back = ring_blocks(grad_resid.astype(LOW), mp_count)

    out_parts = []
    gate_grad_parts = []
    for g, group in enumerate(groups):
        out_g = matmul(hiddens[g], down_one)
        dots = jnp.sum(out_g * cot_rows[g].astype(FULL), axis=1, keepdims=True)
        out_low = (behind(row_gates[g], came) * out_g).astype(LOW)
        out_parts += [p + nought(back[-1]) for p in place(plane_turn(out_low), g)]
        found = lax.dot_general(
            widen.astype(FULL),
            jnp.where(seen[g], dots, 0.0),
            (((0,), (0,)), ((), ())),
            precision=lax.Precision.HIGHEST,
        )
        gate_grad_parts += [
            found[:, k * row_count : (k + 1) * row_count] for k in range(group_size)
        ]
    block_out = (resid + ring_sum(out_parts)).astype(LOW)
    spread = jnp.stack(
        [
            sum(jnp.where(places[b] == p, gate_grad_parts[b], 0.0) for b in blocks)
            for p in range(mp_count)
        ],
        axis=1,
    ).reshape(expert_count, row_count)
    spread = lax.all_to_all(spread, ("dp", "mp"), split_axis=0, concat_axis=0, tiled=True)
    gate_values_grad = jnp.stack(
        [jnp.sum(jnp.where(picked[k], spread, 0.0), axis=0) for k in range(top_count)], axis=1
    )
    inputs_all = joined_rows(inputs)
    late = nought(grad_in)
    down_weight_grad = (contract_first(joined_rows(hiddens), joined_rows(scaled)) + late)[None]
    gate_weight_grad = (contract_first(inputs_all, joined_rows(gate_grads)) + late)[None]
    up_weight_grad = (contract_first(inputs_all, joined_rows(up_grads)) + late)[None]

    out_weight_grad = lax.psum_scatter(
        contract_first(joined_rows(attended), joined_rows(back)).astype(LOW),
        "dp",
        scatter_dimension=1,
        tiled=True,
    ).astype(FULL)
    kv_grads = jnp.zeros((2 * sequence_length, 2 * head_width), FULL)
    query_low, query_gain_part, input_parts = [], 0.0, []
    for b in blocks:
        grad_attended = contract_last(back[b], wo_whole).astype(LOW)
        low_b, kv_b, gain_b = attend_back(
            spots[b],
            queries[b],
            augs[b],
            grad_attended,
            attended[b],
            query_pre[b],
            cosine,
            sine,
            query_gain_row,
            keys_wide,
            values_wide,
            keys_turned,
            score_scale,
        )
        at = places[b] * row_count
        kv_grads = lax.dynamic_update_slice_in_dim(
            kv_grads, lax.dynamic_slice_in_dim(kv_grads, at, kv_b.shape[0], 0) + kv_b, at, 0
        )
        query_low.append(low_b)
        query_gain_part += gain_b[0]
        input_parts.append(contract_last(low_b, wq_whole))
    returned = lax.ppermute(
        kv_grads[:sequence_length].astype(LOW), "dp", [(i + 1, i) for i in range(0, dp_count, 2)]
    )
    kv_total = kv_grads[sequence_length:] + jnp.where(half_index == 0, returned.astype(FULL), 0.0)

    def key_prep(pre, gain):
        normed = rms_norm(pre, gain)
        return normed * cosine + jnp.roll(normed, head_width // 2, axis=1) * sine

    _, key_back = jax.vjp(key_prep, key_pre, key_gain)
    grad_key_pre, key_gain_part = key_back(kv_total[:, :head_width] * score_scale)
    kv_low = jnp.concatenate([grad_key_pre, kv_total[:, head_width:]], axis=1).astype(LOW)
    kv_spread = lax.all_to_all(
        kv_low.reshape(mp_count, row_count, 2 * head_width),
        "mp",
        split_axis=0,
        concat_axis=0,
        tiled=True,
    )
    grad_normed_one = ring_sum(input_parts)
    for m in blocks:
        cols = kv_offsets[m]
        grad_normed_one += contract_last(
            kv_spread[m, :, :head_width], wkv_whole[:, cols : cols + head_width]
        )
        cols += kv_width
        grad_normed_one += contract_last(
            kv_spread[m, :, head_width:], wkv_whole[:, cols : cols + head_width]
        )
    grad_in_norm, input_gain_part = norm_one_back(grad_normed_one)
    tokens_grad = grad_resid + grad_in_norm

    kv_blocks = [
        lax.dynamic_slice_in_dim(kv_low, places[b] * row_count, row_count, 0) for b in blocks
    ]
    sequence_all = joined_rows(sequence)
    kv_part = contract_first(sequence_all, joined_rows(kv_blocks)).astype(LOW)
    weight_part = contract_first(sequence_all, joined_rows(query_low)).astype(LOW)
    half = local_width // 2
    own_cols = lax.all_gather(sum_scatter_rows(kv_part, bits), "mp", axis=0).astype(FULL)
    query_weight_grad = jnp.concatenate(
        [
            sum_scatter_rows(weight_part[:, :half], bits),
            sum_scatter_rows(weight_part[:, half:], bits[:1] + bits[1:][::-1]),
        ],
        axis=1,
    ).astype(FULL)
    kv_parts = [None] * (2 * kv_width // head_width)
    for m in blocks:
        for side in range(2):
            at = (kv_offsets[m] + side * kv_width) // head_width
            term = own_cols[m, :, side * head_width : (side + 1) * head_width]
            kv_parts[at] = term if kv_parts[at] is None else kv_parts[at] + term
    kv_weight_grad = jnp.concatenate(kv_parts, axis=1)

    gains = jnp.concatenate([moe_gain_part, query_gain_part, key_gain_part, input_gain_part])
    for bit in bits:
        gains += swap(gains, "dp", bit)
    step = 1
    while step < mp_count:
        gains += swap(gains, "mp", step)
        step *= 2
    ends = [model_width, model_width + head_width, model_width + 2 * head_width]
    return (
        block_out,
        tokens_grad,
        gains[ends[2] :],
        query_weight_grad,
        kv_weight_grad,
        gains[ends[0] : ends[1]],
        gains[ends[1] : ends[2]],
        out_weight_grad,
        gains[: ends[0]],
        gate_weight_grad,
        up_weight_grad,
        down_weight_grad,
        gate_values_grad,
    )


def solution(mesh):
    both = ("dp", "mp")
    rows = P(both, None)
    experts = P(both, None, None)
    return jax.shard_map(
        on_device,
        mesh=mesh,
        in_specs=(
            rows,
            P(),
            P("dp", "mp"),
            P("dp", None),
            P(),
            P(),
            P("mp", "dp"),
            P(),
            experts,
            experts,
            experts,
            rows,
            rows,
            P(),
            rows,
        ),
        out_specs=(
            rows,
            rows,
            P(),
            P("dp", "mp"),
            P("dp", None),
            P(),
            P(),
            P("mp", "dp"),
            P(),
            experts,
            experts,
            experts,
            rows,
        ),
        check_vma=False,
    )
```

```python
import functools
import math

import jax
import jax.numpy as jnp
from jax import lax
from jax.experimental import pallas as pl
from jax.experimental.layout import Layout, with_layout_constraint
from jax.experimental.pallas import tpu as pltpu
from jax.sharding import PartitionSpec as P

WINDOW = 1024
EPSILON = 1e-06
ROPE_BASE = 1000000.0
FAR = 16384.0
VMEM = 56 * 1024 * 1024
LOW = jnp.bfloat16
FULL = jnp.float32


def rms_norm(value_rows, gain_vector):
    return (
        value_rows
        * lax.rsqrt(jnp.mean(value_rows * value_rows, axis=-1, keepdims=True) + EPSILON)
        * gain_vector
    )


def rope_tables(positions, head_width):
    half_width = head_width // 2
    frequency = jnp.exp(
        jnp.arange(half_width, dtype=FULL) * (-2.0 * math.log(ROPE_BASE) / head_width)
    )
    angles = positions[:, None] * frequency[None, :]
    cosine = jnp.cos(angles)
    sine = jnp.sin(angles)
    return (
        jnp.concatenate([cosine, cosine], axis=-1),
        jnp.concatenate([-sine, sine], axis=-1),
    )


def doc_layout(doc_lengths, sequence_length):
    ends_at = jnp.cumsum(doc_lengths)
    starts_at = ends_at - doc_lengths
    places = jnp.arange(sequence_length, dtype=jnp.int32)
    doc_ids = jnp.sum((places[:, None] >= ends_at[None, :]).astype(jnp.int32), axis=1)
    matches = doc_ids[:, None] == jnp.arange(doc_lengths.shape[0], dtype=jnp.int32)[None, :]
    begins = jnp.sum(jnp.where(matches, starts_at[None, :], 0), axis=1)
    return (doc_ids, places - begins)


def row_major(array):
    return with_layout_constraint(array, Layout(tuple(range(array.ndim))))


def matmul(left, right):
    return jnp.dot(left, right, preferred_element_type=FULL)


def contract_last(left, right):
    return lax.dot_general(left, right, (((1,), (1,)), ((), ())), preferred_element_type=FULL)


def contract_first(left, right):
    return lax.dot_general(left, right, (((0,), (0,)), ((), ())), preferred_element_type=FULL)


def ring_shift(shard, axis="mp"):
    length = lax.axis_size(axis)
    return lax.ppermute(shard, axis, [(i, (i + 1) % length) for i in range(length)])


def swap(shard, axis, bit):
    length = lax.axis_size(axis)
    return lax.ppermute(shard, axis, [(i, i ^ bit) for i in range(length)])


def joined_rows(pieces):
    return pieces[0] if len(pieces) == 1 else jnp.concatenate(pieces, axis=0)


def nought(array):
    return jnp.minimum(jnp.min(jnp.abs(array[:16, :128].astype(FULL))), 0.0)


def pinned(spot, *others):
    return spot + sum(nought(o) for o in others).astype(jnp.int32)


def stage(flag, work):
    shapes = jax.eval_shape(work)
    return lax.cond(
        flag, work, lambda: jax.tree.map(lambda s: jnp.zeros(s.shape, s.dtype), shapes)
    )


def behind(array, *others):
    return (array.astype(FULL) + sum(nought(o) for o in others)).astype(array.dtype)


def sum_scatter_rows(rows, order):
    me = lax.axis_index("dp")
    count = len(order)
    size = rows.shape[0] >> count
    parts = rows.reshape((2,) * count + (size, rows.shape[1]))
    axis_of = {bit: count - bit.bit_length() for bit in order}
    left = sorted(order, reverse=True)
    for bit in order:
        axis = left.index(bit)
        side = (me // bit) % 2
        own = lax.dynamic_index_in_dim(parts, side, axis, keepdims=False)
        other = lax.dynamic_index_in_dim(parts, 1 - side, axis, keepdims=False)
        parts = (own.astype(FULL) + swap(other, "dp", bit).astype(FULL)).astype(LOW)
        left.remove(bit)
    return parts


def ring_sums(parts):
    sums = [parts[1]]
    for b in list(range(2, len(parts))) + [0]:
        sums.append(parts[b] + ring_shift(sums[-1].astype(LOW)).astype(FULL))
    return sums


def far_order(count):
    order = [0]
    for step in range(1, count // 2 + 1):
        order += [step] if 2 * step == count else [step, count - step]
    return order


def shift_by(shard, by, axis="mp"):
    length = lax.axis_size(axis)
    return lax.ppermute(shard, axis, [(i, (i + by) % length) for i in range(length)])


def direct_blocks(shard, count):
    blocks = [shard] + [None] * (count - 1)
    for b in far_order(count)[1:]:
        blocks[b] = shift_by(shard, b)
    return blocks


def ring_blocks(shard, count):
    blocks = [shard]
    for _ in range(1, count):
        blocks.append(ring_shift(blocks[-1]))
    return blocks


def turned(values):
    return pltpu.roll(values, values.shape[1] // 2, axis=1)


def prep_kernel(at_ref, pre_ref, cos_ref, sin_ref, qg_ref, kg_ref, out_ref, kvo_ref):
    width = cos_ref.shape[1]
    cosine, sine = cos_ref[...], sin_ref[...]

    def one(pre, gain):
        rate = lax.rsqrt(jnp.mean(pre * pre, axis=1, keepdims=True) + EPSILON)
        normed = pre * rate * gain
        return (normed * cosine + turned(normed) * sine).astype(LOW)

    wide = out_ref.shape[1]
    for h in range(wide // width):
        cols = slice(h * width, (h + 1) * width)
        out_ref[:, cols] = one(pre_ref[:, cols], qg_ref[...])
    kvo_ref[:, :width] = one(pre_ref[:, wide : wide + width], kg_ref[...])
    kvo_ref[:, width:] = pre_ref[:, wide + width :].astype(LOW)


def prepare(at, pre, wide, cosine, sine, query_gain, key_gain):
    rows = pre.shape[0]
    width = cosine.shape[1]
    step = min(128, rows)
    count = rows // step
    own = lambda i, at: (i, 0)
    table = pl.BlockSpec((step, width), lambda i, at: (at[0] * count + i, 0))
    gain = pl.BlockSpec((1, width), lambda i, at: (0, 0))
    return pl.pallas_call(
        prep_kernel,
        out_shape=(
            jax.ShapeDtypeStruct((rows, wide), LOW),
            jax.ShapeDtypeStruct((rows, 2 * width), LOW),
        ),
        grid_spec=pltpu.PrefetchScalarGridSpec(
            num_scalar_prefetch=1,
            grid=(count,),
            in_specs=[
                pl.BlockSpec((step, pre.shape[1]), own),
                table,
                table,
                gain,
                gain,
            ],
            out_specs=[pl.BlockSpec((step, wide), own), pl.BlockSpec((step, 2 * width), own)],
        ),
        compiler_params=pltpu.CompilerParams(vmem_limit_bytes=VMEM),
        cost_estimate=pl.CostEstimate(flops=1, bytes_accessed=1, transcendentals=0),
    )(at, pre, cosine, sine, query_gain, key_gain)


def thirds(values):
    first = values.astype(LOW)
    rest = values - first.astype(FULL)
    second = rest.astype(LOW)
    return first, second, (rest - second.astype(FULL)).astype(LOW)


def keys_of(kv_ref, ka_ref, part):
    width = ka_ref.shape[1]
    return jnp.concatenate([kv_ref[part, :width], ka_ref[part, :]], axis=1)


def values_of(kv_ref, part):
    values = kv_ref[part, kv_ref.shape[1] // 2 :]
    return jnp.concatenate([values, jnp.ones_like(values)], axis=1)


def attend_kernel(score_scale, docs, at_ref, q_ref, qa_ref, kv_ref, ka_ref, out_ref, aug_ref):
    rows, width = q_ref.shape
    window = WINDOW
    start = pl.multiple_of(at_ref[0] * rows, rows)
    rate = score_scale * math.log2(math.e)
    far = pl.ds(start, rows)
    mid = pl.ds(pl.multiple_of(start + rows, rows), window - rows)
    near = pl.ds(pl.multiple_of(start + window, rows), rows)
    query = jnp.concatenate([q_ref[...], qa_ref[...]], axis=1)
    key_at = lax.broadcasted_iota(jnp.int32, (rows, rows), 1)
    row_at = lax.broadcasted_iota(jnp.int32, (rows, rows), 0)
    upper = key_at > row_at
    corner = jnp.where(
        upper,
        contract_last(query, keys_of(kv_ref, ka_ref, far)),
        contract_last(query, keys_of(kv_ref, ka_ref, near)),
    )
    corner = jnp.exp2(corner * rate)
    total = matmul(jnp.where(upper, corner, 0.0).astype(LOW), values_of(kv_ref, far))
    total += matmul(jnp.where(upper, 0.0, corner).astype(LOW), values_of(kv_ref, near))
    inner = jnp.exp2(contract_last(query, keys_of(kv_ref, ka_ref, mid)) * rate).astype(LOW)
    total += matmul(inner, values_of(kv_ref, mid))
    sums = total[:, width:]
    out_ref[...] = (total[:, :width] / sums).astype(LOW)
    first, second, third = thirds(jnp.log(sums) * (-1.0 / score_scale))
    lane = lax.broadcasted_iota(jnp.int32, (rows, width), 1)
    aug = qa_ref[...].astype(FULL)
    aug = jnp.where(lane == docs + 1, first.astype(FULL), aug)
    aug = jnp.where(lane == docs + 2, second.astype(FULL), aug)
    aug = jnp.where(lane == docs + 3, third.astype(FULL), aug)
    aug_ref[...] = aug.astype(LOW)


def attend(at, queries, query_aug, kv_all, key_aug, score_scale, docs):
    rows, wide = queries.shape
    width = query_aug.shape[1]
    heads = wide // width
    head = pl.BlockSpec((rows, width), lambda h, at: (0, h))
    fixed = lambda array: pl.BlockSpec(array.shape, lambda h, at: (0, 0))
    table = pl.BlockSpec((rows, width), lambda h, at: (at[0], 0))
    return pl.pallas_call(
        functools.partial(attend_kernel, score_scale, docs),
        out_shape=(jax.ShapeDtypeStruct((rows, wide), LOW), jax.ShapeDtypeStruct((rows, wide), LOW)),
        grid_spec=pltpu.PrefetchScalarGridSpec(
            num_scalar_prefetch=1,
            grid=(heads,),
            in_specs=[head, table, fixed(kv_all), fixed(key_aug)],
            out_specs=[head, head],
        ),
        compiler_params=pltpu.CompilerParams(vmem_limit_bytes=VMEM),
        cost_estimate=pl.CostEstimate(flops=1, bytes_accessed=1, transcendentals=0),
    )(at, queries, query_aug, kv_all, key_aug)


def attend_back_kernel(
    score_scale,
    at_ref,
    q_ref,
    qa_ref,
    grad_ref,
    out_ref,
    pre_ref,
    cos_ref,
    sin_ref,
    gain_ref,
    kva_ref,
    ka_ref,
    before_ref,
    low_ref,
    kv_ref,
    gain_grad_ref,
    kt_ref,
):
    rows, width = q_ref.shape
    window = WINDOW
    start = pl.multiple_of(at_ref[0] * rows, rows)
    rate = score_scale * math.log2(math.e)

    @pl.when(pl.program_id(0) == 0)
    def _():
        kv_ref[...] = before_ref[...]
        gain_grad_ref[...] = jnp.zeros_like(gain_grad_ref)
        span = pl.ds(start, rows + window)
        kt_ref[...] = kva_ref[span, :width].astype(FULL).T.astype(LOW)

    query = q_ref[...]
    grad = grad_ref[...]
    query_wide = jnp.concatenate([query, qa_ref[...]], axis=1)
    dots = jnp.sum(grad.astype(FULL) * out_ref[...].astype(FULL), axis=1, keepdims=True)
    first, second, third = thirds(jnp.broadcast_to(-dots, (rows, width)))
    lane = lax.broadcasted_iota(jnp.int32, (rows, width), 1)
    aug = jnp.where(lane == 0, first.astype(FULL), 0.0)
    aug = jnp.where(lane == 1, second.astype(FULL), aug)
    aug = jnp.where(lane == 2, third.astype(FULL), aug)
    grad_wide = jnp.concatenate([grad, aug.astype(LOW)], axis=1)

    def add(part, soft, scores):
        kv_ref[part, :width] += matmul(scores, query)
        kv_ref[part, width:] += matmul(soft, grad)

    mid_size = window - rows
    mid = pl.ds(pl.multiple_of(start + rows, rows), mid_size)
    soft = jnp.exp2(contract_last(keys_of(kva_ref, ka_ref, mid), query_wide) * rate)
    scores = (soft * contract_last(values_of(kva_ref, mid), grad_wide)).astype(LOW)
    add(mid, soft.astype(LOW), scores)
    query_grad = matmul(kt_ref[:, rows:window], scores)

    far = pl.ds(start, rows)
    near = pl.ds(pl.multiple_of(start + window, rows), rows)
    key_at = lax.broadcasted_iota(jnp.int32, (rows, rows), 0)
    row_at = lax.broadcasted_iota(jnp.int32, (rows, rows), 1)
    upper = key_at > row_at
    corner = jnp.where(
        upper,
        contract_last(keys_of(kva_ref, ka_ref, far), query_wide),
        contract_last(keys_of(kva_ref, ka_ref, near), query_wide),
    )
    soft = jnp.exp2(corner * rate)
    slopes = jnp.where(
        upper,
        contract_last(values_of(kva_ref, far), grad_wide),
        contract_last(values_of(kva_ref, near), grad_wide),
    )
    scores = soft * slopes
    scores_far = jnp.where(upper, scores, 0.0).astype(LOW)
    scores_near = jnp.where(upper, 0.0, scores).astype(LOW)
    add(far, jnp.where(upper, soft, 0.0).astype(LOW), scores_far)
    add(near, jnp.where(upper, 0.0, soft).astype(LOW), scores_near)
    query_grad += matmul(kt_ref[:, :rows], scores_far)
    query_grad += matmul(kt_ref[:, window:], scores_near)

    spread = query_grad.T * score_scale
    spread = spread * cos_ref[...] - sin_ref[...] * turned(spread)
    pre = pre_ref[...]
    pace = lax.rsqrt(jnp.mean(pre * pre, axis=1, keepdims=True) + EPSILON)
    normed = pre * pace
    gain_grad_ref[...] += jnp.sum(spread * normed, axis=0, keepdims=True)
    spread = spread * gain_ref[...]
    low_ref[...] = (
        pace * (spread - normed * jnp.mean(spread * normed, axis=1, keepdims=True))
    ).astype(LOW)


def attend_back(
    at, queries, query_aug, grads, outs, pre, cosine, sine, gain, kv_all, key_aug, before, score_scale
):
    rows, wide = queries.shape
    width = cosine.shape[1]
    heads = wide // width
    span = WINDOW + rows
    head = pl.BlockSpec((rows, width), lambda h, at: (0, h))
    fixed = lambda shape: pl.BlockSpec(shape, lambda h, at: (0, 0))
    table = pl.BlockSpec((rows, width), lambda h, at: (at[0], 0))
    return pl.pallas_call(
        functools.partial(attend_back_kernel, score_scale),
        out_shape=(
            jax.ShapeDtypeStruct((rows, wide), LOW),
            jax.ShapeDtypeStruct(before.shape, FULL),
            jax.ShapeDtypeStruct((1, width), FULL),
        ),
        grid_spec=pltpu.PrefetchScalarGridSpec(
            num_scalar_prefetch=1,
            grid=(heads,),
            in_specs=[
                head,
                head,
                head,
                head,
                head,
                table,
                table,
                fixed((1, width)),
                fixed(kv_all.shape),
                fixed(key_aug.shape),
                fixed(before.shape),
            ],
            out_specs=[head, fixed(before.shape), fixed((1, width))],
            scratch_shapes=[pltpu.VMEM((width, span), LOW)],
        ),
        compiler_params=pltpu.CompilerParams(vmem_limit_bytes=VMEM),
        cost_estimate=pl.CostEstimate(flops=1, bytes_accessed=1, transcendentals=0),
    )(at, queries, query_aug, grads, outs, pre, cosine, sine, gain, kv_all, key_aug, before)


def key_back_kernel(
    score_scale, at_ref, kv_ref, more_ref, pre_ref, cos_ref, sin_ref, gain_ref, low_ref, gain_grad_ref
):
    width = cos_ref.shape[1]
    more = jnp.where(at_ref[1] == 0, more_ref[...].astype(FULL), 0.0)
    total = kv_ref[...] + more
    spread = total[:, :width] * score_scale
    spread = spread * cos_ref[...] - sin_ref[...] * turned(spread)
    pre = pre_ref[...]
    pace = lax.rsqrt(jnp.mean(pre * pre, axis=1, keepdims=True) + EPSILON)
    normed = pre * pace
    gain_grad_ref[...] = jnp.sum(spread * normed, axis=0, keepdims=True)
    spread = spread * gain_ref[...]
    low_ref[:, :width] = (
        pace * (spread - normed * jnp.mean(spread * normed, axis=1, keepdims=True))
    ).astype(LOW)
    low_ref[:, width:] = total[:, width:].astype(LOW)


def key_back(spot, half_index, kv_grads, returned, pre, local_width, cosine, sine, gain, score_scale):
    rows = pre.shape[0]
    width = cosine.shape[1]
    ahead = returned.shape[0] // rows
    table = pl.BlockSpec((rows, width), lambda i, at: (at[0], 0))
    return pl.pallas_call(
        functools.partial(key_back_kernel, score_scale),
        out_shape=(
            jax.ShapeDtypeStruct((rows, 2 * width), LOW),
            jax.ShapeDtypeStruct((1, width), FULL),
        ),
        grid_spec=pltpu.PrefetchScalarGridSpec(
            num_scalar_prefetch=1,
            grid=(1,),
            in_specs=[
                pl.BlockSpec((rows, 2 * width), lambda i, at: (at[0] + ahead, 0)),
                pl.BlockSpec((rows, 2 * width), lambda i, at: (at[0], 0)),
                pl.BlockSpec((rows, width), lambda i, at: (0, local_width // width)),
                table,
                table,
                pl.BlockSpec((1, width), lambda i, at: (0, 0)),
            ],
            out_specs=[
                pl.BlockSpec((rows, 2 * width), lambda i, at: (0, 0)),
                pl.BlockSpec((1, width), lambda i, at: (0, 0)),
            ],
        ),
        compiler_params=pltpu.CompilerParams(vmem_limit_bytes=VMEM),
        cost_estimate=pl.CostEstimate(flops=1, bytes_accessed=1, transcendentals=0),
    )(
        jnp.concatenate([spot, half_index.reshape((1,)).astype(jnp.int32)]),
        kv_grads,
        returned,
        pre,
        cosine,
        sine,
        gain,
    )


def on_device(
    tokens,
    input_gain,
    query_weight,
    key_value_weight,
    query_gain,
    key_gain,
    out_weight,
    moe_gain,
    gate_weight,
    up_weight,
    down_weight,
    gate_values,
    routes,
    lengths,
    cotangent,
):
    row_count, model_width = tokens.shape
    head_width = query_gain.shape[0]
    kv_width = key_value_weight.shape[1] // 2
    local_width = query_weight.shape[1]
    local_heads = local_width // head_width
    mp_count = lax.axis_size("mp")
    dp_count = lax.axis_size("dp")
    expert_count = mp_count * dp_count
    heads_per_group = local_heads * mp_count * head_width // kv_width
    kv_offsets = [m * local_heads // heads_per_group * head_width for m in range(mp_count)]
    mp_place = lax.axis_index("mp")
    dp_place = lax.axis_index("dp")
    kv_offset = mp_place * local_heads // heads_per_group * head_width
    sequence_length = row_count * mp_count
    docs = lengths.shape[1]
    score_scale = 1.0 / math.sqrt(head_width)
    half_index = dp_place % 2
    seq_index = dp_place // 2
    shard_rows = query_weight.shape[0]
    blocks = range(mp_count)
    places = [(mp_place - b) % mp_count for b in blocks]
    spots = [p.reshape((1,)).astype(jnp.int32) for p in places]

    resid_in = tokens.astype(FULL)
    normed_one, norm_one_back = jax.vjp(rms_norm, resid_in, input_gain)
    sequence = [normed_one.astype(LOW)]
    for _ in range(1, mp_count - 1):
        sequence.append(ring_shift(sequence[-1]))
    own_whole = lax.all_gather(
        jnp.concatenate(
            [
                query_weight,
                lax.dynamic_slice_in_dim(key_value_weight, kv_offset, head_width, 1),
                lax.dynamic_slice_in_dim(key_value_weight, kv_width + kv_offset, head_width, 1),
            ],
            axis=1,
        ),
        "dp",
        axis=0,
        tiled=True,
    )
    wq_whole = own_whole[:, :local_width]
    wo_whole = lax.all_gather(out_weight, "dp", axis=1, tiled=True)

    top_count = routes.shape[1]
    routed_mean = row_count * top_count // expert_count
    capacity = max(2, routed_mean + routed_mean // 16)
    group_size = 2
    groups = [list(range(b, b + group_size)) for b in range(0, mp_count, group_size)]
    group_rows = group_size * capacity
    bits = [1 << k for k in range(dp_count.bit_length() - 1)]
    routes_turned = routes.T
    gates_turned = gate_values.T
    expert_ids = lax.broadcasted_iota(jnp.int32, (expert_count, row_count), 0)
    picked = [routes_turned[k][None, :] == expert_ids for k in range(top_count)]
    member = sum(p.astype(FULL) for p in picked)
    gate_of = sum(jnp.where(picked[k], gates_turned[k][None, :], 0.0) for k in range(top_count))
    ahead = (
        lax.broadcasted_iota(jnp.int32, (row_count, row_count), 0)
        < lax.broadcasted_iota(jnp.int32, (row_count, row_count), 1)
    ).astype(LOW)
    counts = jnp.where(member > 0, matmul(member.astype(LOW), ahead), -1.0)
    plane_counts = lax.all_to_all(
        counts.astype(LOW).reshape(dp_count, mp_count, row_count).transpose(1, 0, 2),
        "mp",
        split_axis=0,
        concat_axis=0,
        tiled=True,
    )
    expert_view = lax.all_to_all(
        jnp.stack([counts, gate_of], axis=1), ("dp", "mp"), split_axis=0, concat_axis=0, tiled=True
    ).reshape(dp_count, mp_count, 2, row_count)

    row_ids = lax.broadcasted_iota(jnp.int32, (dp_count * group_rows, dp_count), 0)
    widen = (
        row_ids // group_rows == lax.broadcasted_iota(jnp.int32, row_ids.shape, 1)
    ).astype(LOW)
    row_ids = lax.broadcasted_iota(jnp.int32, (dp_count * group_rows, group_size * row_count), 0)
    token_ids = lax.broadcasted_iota(jnp.int32, row_ids.shape, 1)
    aim = jnp.where(
        row_ids % group_rows // capacity == token_ids // row_count, row_ids % capacity, -5
    ).astype(FULL)

    def hot_rows(table):
        return matmul(widen, table.astype(LOW)) == aim

    sends, seen, row_gates = [], [], []
    for group in groups:
        here = jnp.concatenate(
            [lax.dynamic_index_in_dim(plane_counts, places[b], 0, keepdims=False) for b in group],
            axis=1,
        )
        there = jnp.concatenate(
            [lax.dynamic_index_in_dim(expert_view, places[b], 1, keepdims=False) for b in group],
            axis=2,
        )
        sends.append(hot_rows(here).astype(LOW))
        hot = hot_rows(there[:, 0])
        seen.append(hot)
        spread_gates = jnp.dot(
            widen.astype(FULL), there[:, 1], precision=lax.Precision.HIGHEST
        )
        row_gates.append(jnp.sum(jnp.where(hot, spread_gates, 0.0), axis=1, keepdims=True))

    def plane_turn(rows):
        return lax.all_to_all(
            rows.reshape(dp_count, group_rows, model_width),
            "dp",
            split_axis=0,
            concat_axis=0,
            tiled=True,
        ).reshape(dp_count * group_rows, model_width)

    def placed(pieces, g):
        return matmul(sends[g], joined_rows(pieces)).astype(LOW)

    def place(came, g):
        sums = contract_first(sends[g], came)
        return [sums[k * row_count : (k + 1) * row_count] for k in range(group_size)]

    seq_lengths = lax.dynamic_index_in_dim(lengths, seq_index, 0, keepdims=False)
    docs_whole, places_whole = doc_layout(seq_lengths, 2 * sequence_length)
    doc_ids = lax.dynamic_slice_in_dim(docs_whole, half_index * sequence_length, sequence_length, 0)
    positions = lax.dynamic_slice_in_dim(
        places_whole, half_index * sequence_length, sequence_length, 0
    )
    prior_docs = jnp.where(half_index == 1, docs_whole[:sequence_length], -1)
    docs_pad = jnp.concatenate([prior_docs, doc_ids])
    cosine, sine = rope_tables(positions.astype(FULL), head_width)
    lane = jnp.arange(head_width, dtype=jnp.int32)[None, :]
    query_aug = jnp.where(lane < docs, doc_ids[:, None] != lane, lane == docs).astype(LOW)
    key_hit = jnp.where(lane == docs, docs_pad[:, None] == -1, docs_pad[:, None] == lane)
    key_aug = jnp.where(
        lane <= docs, jnp.where(key_hit, -FAR, 0.0), jnp.where(lane <= docs + 3, 1.0, 0.0)
    ).astype(LOW)
    query_gain_row = query_gain.reshape(1, head_width)
    key_gain_row = key_gain.reshape(1, head_width)

    query_pre, queries = [], []
    kv_rows = jnp.zeros((sequence_length, 2 * head_width), LOW)
    for b in blocks:
        if b == mp_count - 1:
            sequence.append(ring_shift(last_sent))
        pre_b = matmul(sequence[b], own_whole)
        queries_b, kv_low = prepare(
            spots[b], pre_b, local_width, cosine, sine, query_gain_row, key_gain_row
        )
        if b == 0:
            last_sent = behind(sequence[mp_count - 2], kv_low)
        if b == 1:
            second_kv = kv_low
        query_pre.append(pre_b)
        queries.append(queries_b)
        kv_rows = lax.dynamic_update_slice_in_dim(kv_rows, kv_low, places[b] * row_count, 0)
    prior = lax.ppermute(kv_rows, "dp", [(i, i + 1) for i in range(0, dp_count, 2)])
    kv_all = jnp.concatenate([prior, kv_rows], axis=0)

    cot_blocks = [cotangent, ring_shift(behind(cotangent, sequence[-1], second_kv))]
    for b in blocks[2:]:
        cot_blocks.append(ring_shift(cot_blocks[-1]))
    cot_rows = []

    attended, augs, head_parts = [None] * mp_count, [None] * mp_count, [None] * mp_count
    for b in list(range(1, mp_count)) + [0]:
        spot = pinned(spots[b], cot_blocks[b]) if b else spots[b]
        attended[b], augs[b] = attend(
            spot, queries[b], query_aug, kv_all, key_aug, score_scale, docs
        )
        head_parts[b] = matmul(attended[b], wo_whole)
    for g, group in enumerate(groups):
        cot_rows.append(plane_turn(placed([cot_blocks[k] for k in group], g)))
    resid = resid_in + ring_sums(head_parts)[-1]
    normed_two, norm_two_back = jax.vjp(rms_norm, resid, moe_gain)

    gate_one, up_one, down_one = gate_weight[0], up_weight[0], down_weight[0]
    normed_blocks = ring_blocks(normed_two.astype(LOW), mp_count)
    kv_all_weights = lax.all_gather(
        behind(own_whole[:, local_width:], normed_blocks[-1]), "mp", axis=1, tiled=True
    )
    inputs, hiddens, scaled, gate_grads, up_grads = [], [], [], [], []
    resid_parts, came = [], None
    for g, group in enumerate(groups):
        rows_g = plane_turn(placed([normed_blocks[b] for b in group], g))
        gate_pre = matmul(rows_g, gate_one)
        up_pre = matmul(rows_g, up_one)
        sigmoid_gate = jax.nn.sigmoid(gate_pre)
        silu_gate = gate_pre * sigmoid_gate
        hidden = (silu_gate * up_pre).astype(LOW)
        scaled_g = (row_gates[g] * cot_rows[g].astype(FULL)).astype(LOW)
        grad_hidden = contract_last(scaled_g, down_one)
        gate_grad = (
            grad_hidden * up_pre * sigmoid_gate * (1.0 + gate_pre * (1.0 - sigmoid_gate))
        ).astype(LOW)
        up_grad = (grad_hidden * silu_gate).astype(LOW)
        grad_in = (contract_last(gate_grad, gate_one) + contract_last(up_grad, up_one)).astype(LOW)
        came = plane_turn(grad_in)
        if group != groups[-1]:
            resid_parts += place(came, g)
        inputs.append(rows_g)
        hiddens.append(hidden)
        scaled.append(scaled_g)
        gate_grads.append(gate_grad)
        up_grads.append(up_grad)
    flag = routes[0, 0] >= 0
    last = groups[-1]
    sums = [resid_parts[1]]
    for b in range(2, last[0]):
        sums.append(resid_parts[b] + ring_shift(sums[-1].astype(LOW)).astype(FULL))
    passed = ring_shift(sums[-1].astype(LOW))
    late = nought(sums[0])
    pairs = [(hiddens, scaled), (inputs, gate_grads), (inputs, up_grads)]
    weight_parts = []
    for left, right in pairs:
        part = late
        for g in range(len(groups) - 1):
            part = row_major(contract_first(left[g], right[g]) + part)
        weight_parts.append(part)

    def expert_outs(g, tie):
        out_g = matmul(hiddens[g], down_one)
        dots = jnp.sum(out_g * cot_rows[g].astype(FULL), axis=1, keepdims=True)
        found = lax.dot_general(
            widen.astype(FULL),
            jnp.where(seen[g], dots, 0.0),
            (((0,), (0,)), ((), ())),
            precision=lax.Precision.HIGHEST,
        )
        return ((row_gates[g] + tie) * out_g).astype(LOW), found

    outs = [expert_outs(g, late) for g in range(len(groups) - 1)]
    own_part = resid_parts[0]

    def sum_work():
        first_out = plane_turn(outs[0][0])
        parts = place(came, len(groups) - 1)
        total = parts[0] + passed.astype(FULL)
        for part in parts[1:] + [own_part]:
            total = part + ring_shift(total.astype(LOW)).astype(FULL)
        grad_norm, gain_part = norm_two_back(total)
        grad = cotangent.astype(FULL) + grad_norm
        return (
            grad,
            grad.astype(LOW),
            gain_part,
            first_out,
            [
                row_major(contract_first(left[-1], right[-1]) + part)
                for (left, right), part in zip(pairs, weight_parts)
            ],
            expert_outs(len(groups) - 1, 0.0),
        )

    grad_resid, back_own, moe_gain_part, first_out, weight_grads, last_outs = stage(flag, sum_work)
    down_weight_grad, gate_weight_grad, up_weight_grad = weight_grads
    outs.append(last_outs)
    back = [back_own]
    out_came = [first_out] + [plane_turn(rows) for rows, _ in outs[1:]]
    gate_grad_parts = [
        found[:, k * row_count : (k + 1) * row_count] for _, found in outs for k in range(group_size)
    ]

    kv_grads = jnp.zeros((2 * sequence_length, 2 * head_width), FULL)
    query_low, input_parts = [], []
    query_gain_part = 0.0
    for b in blocks:
        ended = b == mp_count - 1
        spot = pinned(spots[b], *out_came[1:]) if ended else spots[b]

        def block_work():
            extra = ()
            if not ended:
                extra += (ring_shift(back[b]),)
            else:
                extra += (ring_shift(input_parts[1].astype(LOW)),)
                out_part = place(out_came[0], 0)
                extra += (out_part[0], ring_shift(out_part[1].astype(LOW)))
                extra += (contract_first(joined_rows(attended), joined_rows(back)).astype(LOW),)
            if b == 0:
                spread = jnp.stack(
                    [
                        sum(jnp.where(places[k] == p, gate_grad_parts[k], 0.0) for k in blocks)
                        for p in blocks
                    ],
                    axis=1,
                ).reshape(expert_count, row_count)
                extra += (
                    lax.all_to_all(spread, ("dp", "mp"), split_axis=0, concat_axis=0, tiled=True),
                )
            low, kv, gain = attend_back(
                spot,
                queries[b],
                augs[b],
                contract_last(back[b], wo_whole).astype(LOW),
                attended[b],
                query_pre[b],
                cosine,
                sine,
                query_gain_row,
                kv_all,
                key_aug,
                kv_grads,
                score_scale,
            )
            return (low, kv, gain, contract_last(low, wq_whole)) + extra

        low_b, kv_b, gain_b, input_b, *extra = stage(flag, block_work)
        kv_grads = kv_b
        query_low.append(low_b)
        input_parts.append(input_b)
        query_gain_part += gain_b[0]
        if not ended:
            back.append(extra[0])
        if b == 0:
            spread = extra[1]
    input_passed, out_own, out_passed, out_weight_part = extra
    gate_values_grad = jnp.stack(
        [jnp.sum(jnp.where(picked[k], spread, 0.0), axis=0) for k in range(top_count)], axis=1
    )

    def dp_turn(parts):
        return lax.all_to_all(parts, "dp", split_axis=0, concat_axis=0, tiled=True)

    out_weight_grad = lax.psum_scatter(
        out_weight_part, "dp", scatter_dimension=1, tiled=True
    ).astype(FULL)
    sequence_all = joined_rows(sequence)

    def input_work():
        weight_part = row_major(contract_first(sequence_all, joined_rows(query_low)).astype(LOW))
        weight_came = dp_turn(weight_part.reshape(dp_count, shard_rows, local_width))
        returned = lax.ppermute(
            kv_grads[:sequence_length].astype(LOW),
            "dp",
            [(i + 1, i) for i in range(0, dp_count, 2)],
        )
        total = input_parts[2] + input_passed.astype(FULL)
        for part in input_parts[3:] + [input_parts[0]]:
            total = part + ring_shift(total.astype(LOW)).astype(FULL)
        kv_blocks, key_gain_part = [], 0.0
        for b in blocks:
            kv_low, gain_b = key_back(
                spots[b],
                half_index,
                kv_grads,
                returned,
                query_pre[b],
                local_width,
                cosine,
                sine,
                key_gain_row,
                score_scale,
            )
            kv_blocks.append(kv_low)
            key_gain_part += gain_b[0]
        kv_spread = jnp.zeros((mp_count, row_count, 2 * head_width), LOW)
        for b in blocks:
            kv_came = shift_by(kv_blocks[b], -b) if b else kv_blocks[0]
            kv_spread = lax.dynamic_update_index_in_dim(
                kv_spread, kv_came, (mp_place + b) % mp_count, 0
            )
        total += lax.dot_general(
            kv_spread.transpose(1, 0, 2).reshape(row_count, -1),
            kv_all_weights,
            (((1,), (1,)), ((), ())),
            preferred_element_type=FULL,
        )
        out_parts = []
        for g in range(1, len(groups)):
            out_parts += place(out_came[g], g)
        return (
            row_major(weight_came),
            total,
            key_gain_part,
            row_major(contract_first(sequence_all, joined_rows(kv_blocks)).astype(LOW)),
            out_parts,
        )

    weight_came, grad_normed_one, key_gain_part, kv_part, out_parts = stage(flag, input_work)
    out_total = out_parts[0] + out_passed.astype(FULL)
    for part in out_parts[1:] + [out_own]:
        out_total = part + ring_shift(out_total.astype(LOW)).astype(FULL)
    block_out = (resid + out_total).astype(LOW)
    grad_in_norm, input_gain_part = norm_one_back(grad_normed_one)
    tokens_grad = grad_resid + grad_in_norm

    query_weight_grad = jnp.sum(weight_came.astype(FULL), axis=0)
    own_cols = lax.all_gather(sum_scatter_rows(kv_part, bits), "mp", axis=0).astype(FULL)
    kv_parts = [None] * (2 * kv_width // head_width)
    for m in blocks:
        for side in range(2):
            at = (kv_offsets[m] + side * kv_width) // head_width
            term = own_cols[m, :, side * head_width : (side + 1) * head_width]
            kv_parts[at] = term if kv_parts[at] is None else kv_parts[at] + term
    kv_weight_grad = jnp.concatenate(kv_parts, axis=1)

    gains = jnp.concatenate([moe_gain_part, query_gain_part, key_gain_part, input_gain_part])
    for bit in bits:
        gains += swap(gains, "dp", bit)
    step = 1
    while step < mp_count:
        gains += swap(gains, "mp", step)
        step *= 2
    ends = [model_width, model_width + head_width, model_width + 2 * head_width]
    return (
        block_out,
        tokens_grad,
        gains[ends[2] :],
        query_weight_grad,
        kv_weight_grad,
        gains[ends[0] : ends[1]],
        gains[ends[1] : ends[2]],
        out_weight_grad,
        gains[: ends[0]],
        gate_weight_grad[None],
        up_weight_grad[None],
        down_weight_grad[None],
        gate_values_grad,
    )


def solution(mesh):
    both = ("dp", "mp")
    rows = P(both, None)
    experts = P(both, None, None)
    return jax.shard_map(
        on_device,
        mesh=mesh,
        in_specs=(
            rows,
            P(),
            P("dp", "mp"),
            P("dp", None),
            P(),
            P(),
            P("mp", "dp"),
            P(),
            experts,
            experts,
            experts,
            rows,
            rows,
            P(),
            rows,
        ),
        out_specs=(
            rows,
            rows,
            P(),
            P("dp", "mp"),
            P("dp", None),
            P(),
            P(),
            P("mp", "dp"),
            P(),
            experts,
            experts,
            experts,
            rows,
        ),
        check_vma=False,
    )
```

```python
import functools
import math

import jax
import jax.numpy as jnp
from jax import lax
from jax.experimental import pallas as pl
from jax.experimental.layout import Layout, with_layout_constraint
from jax.experimental.pallas import tpu as pltpu
from jax.sharding import PartitionSpec as P

WINDOW = 1024
EPSILON = 1e-06
ROPE_BASE = 1000000.0
FAR = 16384.0
VMEM = 56 * 1024 * 1024
LOW = jnp.bfloat16
FULL = jnp.float32


def rms_norm(value_rows, gain_vector):
    return (
        value_rows
        * lax.rsqrt(jnp.mean(value_rows * value_rows, axis=-1, keepdims=True) + EPSILON)
        * gain_vector
    )


def rope_tables(positions, head_width):
    half_width = head_width // 2
    frequency = jnp.exp(
        jnp.arange(half_width, dtype=FULL) * (-2.0 * math.log(ROPE_BASE) / head_width)
    )
    angles = positions[:, None] * frequency[None, :]
    cosine = jnp.cos(angles)
    sine = jnp.sin(angles)
    return (
        jnp.concatenate([cosine, cosine], axis=-1),
        jnp.concatenate([-sine, sine], axis=-1),
    )


def doc_layout(doc_lengths, sequence_length):
    ends_at = jnp.cumsum(doc_lengths)
    starts_at = ends_at - doc_lengths
    places = jnp.arange(sequence_length, dtype=jnp.int32)
    doc_ids = jnp.sum((places[:, None] >= ends_at[None, :]).astype(jnp.int32), axis=1)
    matches = doc_ids[:, None] == jnp.arange(doc_lengths.shape[0], dtype=jnp.int32)[None, :]
    begins = jnp.sum(jnp.where(matches, starts_at[None, :], 0), axis=1)
    return (doc_ids, places - begins)


def row_major(array):
    return with_layout_constraint(array, Layout(tuple(range(array.ndim))))


def matmul(left, right):
    return jnp.dot(left, right, preferred_element_type=FULL)


def contract_last(left, right):
    return lax.dot_general(left, right, (((1,), (1,)), ((), ())), preferred_element_type=FULL)


def contract_first(left, right):
    return lax.dot_general(left, right, (((0,), (0,)), ((), ())), preferred_element_type=FULL)


def ring_shift(shard, axis="mp"):
    length = lax.axis_size(axis)
    return lax.ppermute(shard, axis, [(i, (i + 1) % length) for i in range(length)])


def swap(shard, axis, bit):
    length = lax.axis_size(axis)
    return lax.ppermute(shard, axis, [(i, i ^ bit) for i in range(length)])


def joined_rows(pieces):
    return pieces[0] if len(pieces) == 1 else jnp.concatenate(pieces, axis=0)


def nought(array):
    return jnp.minimum(jnp.min(jnp.abs(array[:16, :128].astype(FULL))), 0.0)


def pinned(spot, *others):
    return spot + sum(nought(o) for o in others).astype(jnp.int32)


def stage(flag, work):
    shapes = jax.eval_shape(work)
    return lax.cond(
        flag, work, lambda: jax.tree.map(lambda s: jnp.zeros(s.shape, s.dtype), shapes)
    )


def behind(array, *others):
    return (array.astype(FULL) + sum(nought(o) for o in others)).astype(array.dtype)


def half_rows(rows, bit):
    side = (lax.axis_index("dp") // bit) % 2
    size = lax.axis_size("dp")
    parts = rows.reshape((-1, 2, rows.shape[0] * bit // size, rows.shape[1]))
    own = lax.dynamic_index_in_dim(parts, side, 1, keepdims=False)
    other = lax.dynamic_index_in_dim(parts, 1 - side, 1, keepdims=False)
    total = own.astype(FULL) + swap(other, "dp", bit).astype(FULL)
    return total.astype(LOW).reshape((-1, rows.shape[1]))


def ring_sums(parts):
    sums = [parts[1]]
    for b in list(range(2, len(parts))) + [0]:
        sums.append(parts[b] + ring_shift(sums[-1].astype(LOW)).astype(FULL))
    return sums


def far_order(count):
    order = [0]
    for step in range(1, count // 2 + 1):
        order += [step] if 2 * step == count else [step, count - step]
    return order


def shift_by(shard, by, axis="mp"):
    length = lax.axis_size(axis)
    return lax.ppermute(shard, axis, [(i, (i + by) % length) for i in range(length)])


def direct_blocks(shard, count):
    blocks = [shard] + [None] * (count - 1)
    for b in far_order(count)[1:]:
        blocks[b] = shift_by(shard, b)
    return blocks


def ring_blocks(shard, count):
    blocks = [shard]
    for _ in range(1, count):
        blocks.append(ring_shift(blocks[-1]))
    return blocks


def turned(values):
    return pltpu.roll(values, values.shape[1] // 2, axis=1)


def prep_kernel(at_ref, pre_ref, cos_ref, sin_ref, qg_ref, kg_ref, out_ref, kvo_ref):
    width = cos_ref.shape[1]
    cosine, sine = cos_ref[...], sin_ref[...]

    def one(pre, gain):
        rate = lax.rsqrt(jnp.mean(pre * pre, axis=1, keepdims=True) + EPSILON)
        normed = pre * rate * gain
        return (normed * cosine + turned(normed) * sine).astype(LOW)

    wide = out_ref.shape[1]
    for h in range(wide // width):
        cols = slice(h * width, (h + 1) * width)
        out_ref[:, cols] = one(pre_ref[:, cols], qg_ref[...])
    kvo_ref[:, :width] = one(pre_ref[:, wide : wide + width], kg_ref[...])
    kvo_ref[:, width:] = pre_ref[:, wide + width :].astype(LOW)


def prepare(at, pre, wide, cosine, sine, query_gain, key_gain):
    rows = pre.shape[0]
    width = cosine.shape[1]
    step = min(128, rows)
    count = rows // step
    own = lambda i, at: (i, 0)
    table = pl.BlockSpec((step, width), lambda i, at: (at[0] * count + i, 0))
    gain = pl.BlockSpec((1, width), lambda i, at: (0, 0))
    return pl.pallas_call(
        prep_kernel,
        out_shape=(
            jax.ShapeDtypeStruct((rows, wide), LOW),
            jax.ShapeDtypeStruct((rows, 2 * width), LOW),
        ),
        grid_spec=pltpu.PrefetchScalarGridSpec(
            num_scalar_prefetch=1,
            grid=(count,),
            in_specs=[
                pl.BlockSpec((step, pre.shape[1]), own),
                table,
                table,
                gain,
                gain,
            ],
            out_specs=[pl.BlockSpec((step, wide), own), pl.BlockSpec((step, 2 * width), own)],
        ),
        compiler_params=pltpu.CompilerParams(vmem_limit_bytes=VMEM),
        cost_estimate=pl.CostEstimate(flops=1, bytes_accessed=1, transcendentals=0),
    )(at, pre, cosine, sine, query_gain, key_gain)


def thirds(values):
    first = values.astype(LOW)
    rest = values - first.astype(FULL)
    second = rest.astype(LOW)
    return first, second, (rest - second.astype(FULL)).astype(LOW)


def keys_of(kv_ref, ka_ref, part):
    width = ka_ref.shape[1]
    return jnp.concatenate([kv_ref[part, :width], ka_ref[part, :]], axis=1)


def values_of(kv_ref, part):
    values = kv_ref[part, kv_ref.shape[1] // 2 :]
    return jnp.concatenate([values, jnp.ones_like(values)], axis=1)


def attend_kernel(score_scale, docs, at_ref, q_ref, qa_ref, kv_ref, ka_ref, out_ref, aug_ref):
    rows, width = q_ref.shape
    window = WINDOW
    start = pl.multiple_of(at_ref[0] * rows, rows)
    rate = score_scale * math.log2(math.e)
    far = pl.ds(start, rows)
    mid = pl.ds(pl.multiple_of(start + rows, rows), window - rows)
    near = pl.ds(pl.multiple_of(start + window, rows), rows)
    query = jnp.concatenate([q_ref[...], qa_ref[...]], axis=1)
    key_at = lax.broadcasted_iota(jnp.int32, (rows, rows), 1)
    row_at = lax.broadcasted_iota(jnp.int32, (rows, rows), 0)
    upper = key_at > row_at
    corner = jnp.where(
        upper,
        contract_last(query, keys_of(kv_ref, ka_ref, far)),
        contract_last(query, keys_of(kv_ref, ka_ref, near)),
    )
    corner = jnp.exp2(corner * rate)
    total = matmul(jnp.where(upper, corner, 0.0).astype(LOW), values_of(kv_ref, far))
    total += matmul(jnp.where(upper, 0.0, corner).astype(LOW), values_of(kv_ref, near))
    inner = jnp.exp2(contract_last(query, keys_of(kv_ref, ka_ref, mid)) * rate).astype(LOW)
    total += matmul(inner, values_of(kv_ref, mid))
    sums = total[:, width:]
    out_ref[...] = (total[:, :width] / sums).astype(LOW)
    first, second, third = thirds(jnp.log(sums) * (-1.0 / score_scale))
    lane = lax.broadcasted_iota(jnp.int32, (rows, width), 1)
    aug = qa_ref[...].astype(FULL)
    aug = jnp.where(lane == docs + 1, first.astype(FULL), aug)
    aug = jnp.where(lane == docs + 2, second.astype(FULL), aug)
    aug = jnp.where(lane == docs + 3, third.astype(FULL), aug)
    aug_ref[...] = aug.astype(LOW)


def attend(at, queries, query_aug, kv_all, key_aug, score_scale, docs):
    rows, wide = queries.shape
    width = query_aug.shape[1]
    heads = wide // width
    head = pl.BlockSpec((rows, width), lambda h, at: (0, h))
    fixed = lambda array: pl.BlockSpec(array.shape, lambda h, at: (0, 0))
    table = pl.BlockSpec((rows, width), lambda h, at: (at[0], 0))
    return pl.pallas_call(
        functools.partial(attend_kernel, score_scale, docs),
        out_shape=(jax.ShapeDtypeStruct((rows, wide), LOW), jax.ShapeDtypeStruct((rows, wide), LOW)),
        grid_spec=pltpu.PrefetchScalarGridSpec(
            num_scalar_prefetch=1,
            grid=(heads,),
            in_specs=[head, table, fixed(kv_all), fixed(key_aug)],
            out_specs=[head, head],
        ),
        compiler_params=pltpu.CompilerParams(vmem_limit_bytes=VMEM),
        cost_estimate=pl.CostEstimate(flops=1, bytes_accessed=1, transcendentals=0),
    )(at, queries, query_aug, kv_all, key_aug)


def attend_back_kernel(
    score_scale,
    at_ref,
    q_ref,
    qa_ref,
    grad_ref,
    out_ref,
    pre_ref,
    cos_ref,
    sin_ref,
    gain_ref,
    kva_ref,
    ka_ref,
    before_ref,
    low_ref,
    kv_ref,
    gain_grad_ref,
    kt_ref,
):
    rows, width = q_ref.shape
    window = WINDOW
    start = pl.multiple_of(at_ref[0] * rows, rows)
    rate = score_scale * math.log2(math.e)

    @pl.when(pl.program_id(0) == 0)
    def _():
        kv_ref[...] = before_ref[...]
        gain_grad_ref[...] = jnp.zeros_like(gain_grad_ref)
        span = pl.ds(start, rows + window)
        kt_ref[...] = kva_ref[span, :width].astype(FULL).T.astype(LOW)

    query = q_ref[...]
    grad = grad_ref[...]
    query_wide = jnp.concatenate([query, qa_ref[...]], axis=1)
    dots = jnp.sum(grad.astype(FULL) * out_ref[...].astype(FULL), axis=1, keepdims=True)
    first, second, third = thirds(jnp.broadcast_to(-dots, (rows, width)))
    lane = lax.broadcasted_iota(jnp.int32, (rows, width), 1)
    aug = jnp.where(lane == 0, first.astype(FULL), 0.0)
    aug = jnp.where(lane == 1, second.astype(FULL), aug)
    aug = jnp.where(lane == 2, third.astype(FULL), aug)
    grad_wide = jnp.concatenate([grad, aug.astype(LOW)], axis=1)

    def add(part, soft, scores):
        kv_ref[part, :width] += matmul(scores, query)
        kv_ref[part, width:] += matmul(soft, grad)

    mid_size = window - rows
    mid = pl.ds(pl.multiple_of(start + rows, rows), mid_size)
    soft = jnp.exp2(contract_last(keys_of(kva_ref, ka_ref, mid), query_wide) * rate)
    scores = (soft * contract_last(values_of(kva_ref, mid), grad_wide)).astype(LOW)
    add(mid, soft.astype(LOW), scores)
    query_grad = matmul(kt_ref[:, rows:window], scores)

    far = pl.ds(start, rows)
    near = pl.ds(pl.multiple_of(start + window, rows), rows)
    key_at = lax.broadcasted_iota(jnp.int32, (rows, rows), 0)
    row_at = lax.broadcasted_iota(jnp.int32, (rows, rows), 1)
    upper = key_at > row_at
    corner = jnp.where(
        upper,
        contract_last(keys_of(kva_ref, ka_ref, far), query_wide),
        contract_last(keys_of(kva_ref, ka_ref, near), query_wide),
    )
    soft = jnp.exp2(corner * rate)
    slopes = jnp.where(
        upper,
        contract_last(values_of(kva_ref, far), grad_wide),
        contract_last(values_of(kva_ref, near), grad_wide),
    )
    scores = soft * slopes
    scores_far = jnp.where(upper, scores, 0.0).astype(LOW)
    scores_near = jnp.where(upper, 0.0, scores).astype(LOW)
    add(far, jnp.where(upper, soft, 0.0).astype(LOW), scores_far)
    add(near, jnp.where(upper, 0.0, soft).astype(LOW), scores_near)
    query_grad += matmul(kt_ref[:, :rows], scores_far)
    query_grad += matmul(kt_ref[:, window:], scores_near)

    spread = query_grad.T * score_scale
    spread = spread * cos_ref[...] - sin_ref[...] * turned(spread)
    pre = pre_ref[...]
    pace = lax.rsqrt(jnp.mean(pre * pre, axis=1, keepdims=True) + EPSILON)
    normed = pre * pace
    gain_grad_ref[...] += jnp.sum(spread * normed, axis=0, keepdims=True)
    spread = spread * gain_ref[...]
    low_ref[...] = (
        pace * (spread - normed * jnp.mean(spread * normed, axis=1, keepdims=True))
    ).astype(LOW)


def attend_back(
    at, queries, query_aug, grads, outs, pre, cosine, sine, gain, kv_all, key_aug, before, score_scale
):
    rows, wide = queries.shape
    width = cosine.shape[1]
    heads = wide // width
    span = WINDOW + rows
    head = pl.BlockSpec((rows, width), lambda h, at: (0, h))
    fixed = lambda shape: pl.BlockSpec(shape, lambda h, at: (0, 0))
    table = pl.BlockSpec((rows, width), lambda h, at: (at[0], 0))
    return pl.pallas_call(
        functools.partial(attend_back_kernel, score_scale),
        out_shape=(
            jax.ShapeDtypeStruct((rows, wide), LOW),
            jax.ShapeDtypeStruct(before.shape, FULL),
            jax.ShapeDtypeStruct((1, width), FULL),
        ),
        grid_spec=pltpu.PrefetchScalarGridSpec(
            num_scalar_prefetch=1,
            grid=(heads,),
            in_specs=[
                head,
                head,
                head,
                head,
                head,
                table,
                table,
                fixed((1, width)),
                fixed(kv_all.shape),
                fixed(key_aug.shape),
                fixed(before.shape),
            ],
            out_specs=[head, fixed(before.shape), fixed((1, width))],
            scratch_shapes=[pltpu.VMEM((width, span), LOW)],
        ),
        compiler_params=pltpu.CompilerParams(vmem_limit_bytes=VMEM),
        cost_estimate=pl.CostEstimate(flops=1, bytes_accessed=1, transcendentals=0),
    )(at, queries, query_aug, grads, outs, pre, cosine, sine, gain, kv_all, key_aug, before)


def key_back_kernel(
    score_scale, at_ref, kv_ref, more_ref, pre_ref, cos_ref, sin_ref, gain_ref, low_ref, gain_grad_ref
):
    width = cos_ref.shape[1]
    more = jnp.where(at_ref[1] == 0, more_ref[...].astype(FULL), 0.0)
    total = kv_ref[...] + more
    spread = total[:, :width] * score_scale
    spread = spread * cos_ref[...] - sin_ref[...] * turned(spread)
    pre = pre_ref[...]
    pace = lax.rsqrt(jnp.mean(pre * pre, axis=1, keepdims=True) + EPSILON)
    normed = pre * pace
    gain_grad_ref[...] = jnp.sum(spread * normed, axis=0, keepdims=True)
    spread = spread * gain_ref[...]
    low_ref[:, :width] = (
        pace * (spread - normed * jnp.mean(spread * normed, axis=1, keepdims=True))
    ).astype(LOW)
    low_ref[:, width:] = total[:, width:].astype(LOW)


def key_back(spot, half_index, kv_grads, returned, pre, local_width, cosine, sine, gain, score_scale):
    rows = pre.shape[0]
    width = cosine.shape[1]
    ahead = returned.shape[0] // rows
    table = pl.BlockSpec((rows, width), lambda i, at: (at[0], 0))
    return pl.pallas_call(
        functools.partial(key_back_kernel, score_scale),
        out_shape=(
            jax.ShapeDtypeStruct((rows, 2 * width), LOW),
            jax.ShapeDtypeStruct((1, width), FULL),
        ),
        grid_spec=pltpu.PrefetchScalarGridSpec(
            num_scalar_prefetch=1,
            grid=(1,),
            in_specs=[
                pl.BlockSpec((rows, 2 * width), lambda i, at: (at[0] + ahead, 0)),
                pl.BlockSpec((rows, 2 * width), lambda i, at: (at[0], 0)),
                pl.BlockSpec((rows, width), lambda i, at: (0, local_width // width)),
                table,
                table,
                pl.BlockSpec((1, width), lambda i, at: (0, 0)),
            ],
            out_specs=[
                pl.BlockSpec((rows, 2 * width), lambda i, at: (0, 0)),
                pl.BlockSpec((1, width), lambda i, at: (0, 0)),
            ],
        ),
        compiler_params=pltpu.CompilerParams(vmem_limit_bytes=VMEM),
        cost_estimate=pl.CostEstimate(flops=1, bytes_accessed=1, transcendentals=0),
    )(
        jnp.concatenate([spot, half_index.reshape((1,)).astype(jnp.int32)]),
        kv_grads,
        returned,
        pre,
        cosine,
        sine,
        gain,
    )


def on_device(
    tokens,
    input_gain,
    query_weight,
    key_value_weight,
    query_gain,
    key_gain,
    out_weight,
    moe_gain,
    gate_weight,
    up_weight,
    down_weight,
    gate_values,
    routes,
    lengths,
    cotangent,
):
    row_count, model_width = tokens.shape
    head_width = query_gain.shape[0]
    kv_width = key_value_weight.shape[1] // 2
    local_width = query_weight.shape[1]
    local_heads = local_width // head_width
    mp_count = lax.axis_size("mp")
    dp_count = lax.axis_size("dp")
    expert_count = mp_count * dp_count
    heads_per_group = local_heads * mp_count * head_width // kv_width
    kv_offsets = [m * local_heads // heads_per_group * head_width for m in range(mp_count)]
    mp_place = lax.axis_index("mp")
    dp_place = lax.axis_index("dp")
    kv_offset = mp_place * local_heads // heads_per_group * head_width
    sequence_length = row_count * mp_count
    docs = lengths.shape[1]
    score_scale = 1.0 / math.sqrt(head_width)
    half_index = dp_place % 2
    seq_index = dp_place // 2
    shard_rows = query_weight.shape[0]
    blocks = range(mp_count)
    places = [(mp_place - b) % mp_count for b in blocks]
    spots = [p.reshape((1,)).astype(jnp.int32) for p in places]

    resid_in = tokens.astype(FULL)
    normed_one, norm_one_back = jax.vjp(rms_norm, resid_in, input_gain)
    sequence = [normed_one.astype(LOW)]
    for _ in range(1, mp_count - 1):
        sequence.append(ring_shift(sequence[-1]))
    own_whole = lax.all_gather(
        jnp.concatenate(
            [
                query_weight,
                lax.dynamic_slice_in_dim(key_value_weight, kv_offset, head_width, 1),
                lax.dynamic_slice_in_dim(key_value_weight, kv_width + kv_offset, head_width, 1),
            ],
            axis=1,
        ),
        "dp",
        axis=0,
        tiled=True,
    )
    wq_whole = own_whole[:, :local_width]
    wo_whole = lax.all_gather(out_weight, "dp", axis=1, tiled=True)

    top_count = routes.shape[1]
    routed_mean = row_count * top_count // expert_count
    capacity = max(2, routed_mean + routed_mean // 16)
    group_size = 2
    groups = [list(range(b, b + group_size)) for b in range(0, mp_count, group_size)]
    group_rows = group_size * capacity
    bits = [1 << k for k in range(dp_count.bit_length() - 1)]
    routes_turned = routes.T
    gates_turned = gate_values.T
    expert_ids = lax.broadcasted_iota(jnp.int32, (expert_count, row_count), 0)
    picked = [routes_turned[k][None, :] == expert_ids for k in range(top_count)]
    member = sum(p.astype(FULL) for p in picked)
    gate_of = sum(jnp.where(picked[k], gates_turned[k][None, :], 0.0) for k in range(top_count))
    ahead = (
        lax.broadcasted_iota(jnp.int32, (row_count, row_count), 0)
        < lax.broadcasted_iota(jnp.int32, (row_count, row_count), 1)
    ).astype(LOW)
    counts = jnp.where(member > 0, matmul(member.astype(LOW), ahead), -1.0)
    plane_counts = lax.all_to_all(
        counts.astype(LOW).reshape(dp_count, mp_count, row_count).transpose(1, 0, 2),
        "mp",
        split_axis=0,
        concat_axis=0,
        tiled=True,
    )
    expert_view = lax.all_to_all(
        jnp.stack([counts, gate_of], axis=1), ("dp", "mp"), split_axis=0, concat_axis=0, tiled=True
    ).reshape(dp_count, mp_count, 2, row_count)

    row_ids = lax.broadcasted_iota(jnp.int32, (dp_count * group_rows, dp_count), 0)
    widen = (
        row_ids // group_rows == lax.broadcasted_iota(jnp.int32, row_ids.shape, 1)
    ).astype(LOW)
    row_ids = lax.broadcasted_iota(jnp.int32, (dp_count * group_rows, group_size * row_count), 0)
    token_ids = lax.broadcasted_iota(jnp.int32, row_ids.shape, 1)
    aim = jnp.where(
        row_ids % group_rows // capacity == token_ids // row_count, row_ids % capacity, -5
    ).astype(FULL)

    def hot_rows(table):
        return matmul(widen, table.astype(LOW)) == aim

    sends, seen, row_gates = [], [], []
    for group in groups:
        here = jnp.concatenate(
            [lax.dynamic_index_in_dim(plane_counts, places[b], 0, keepdims=False) for b in group],
            axis=1,
        )
        there = jnp.concatenate(
            [lax.dynamic_index_in_dim(expert_view, places[b], 1, keepdims=False) for b in group],
            axis=2,
        )
        sends.append(hot_rows(here).astype(LOW))
        hot = hot_rows(there[:, 0])
        seen.append(hot)
        spread_gates = jnp.dot(
            widen.astype(FULL), there[:, 1], precision=lax.Precision.HIGHEST
        )
        row_gates.append(jnp.sum(jnp.where(hot, spread_gates, 0.0), axis=1, keepdims=True))

    def plane_turn(rows):
        return lax.all_to_all(
            rows.reshape(dp_count, group_rows, model_width),
            "dp",
            split_axis=0,
            concat_axis=0,
            tiled=True,
        ).reshape(dp_count * group_rows, model_width)

    def placed(pieces, g):
        return matmul(sends[g], joined_rows(pieces)).astype(LOW)

    def place(came, g):
        sums = contract_first(sends[g], came)
        return [sums[k * row_count : (k + 1) * row_count] for k in range(group_size)]

    seq_lengths = lax.dynamic_index_in_dim(lengths, seq_index, 0, keepdims=False)
    docs_whole, places_whole = doc_layout(seq_lengths, 2 * sequence_length)
    doc_ids = lax.dynamic_slice_in_dim(docs_whole, half_index * sequence_length, sequence_length, 0)
    positions = lax.dynamic_slice_in_dim(
        places_whole, half_index * sequence_length, sequence_length, 0
    )
    prior_docs = jnp.where(half_index == 1, docs_whole[:sequence_length], -1)
    docs_pad = jnp.concatenate([prior_docs, doc_ids])
    cosine, sine = rope_tables(positions.astype(FULL), head_width)
    lane = jnp.arange(head_width, dtype=jnp.int32)[None, :]
    query_aug = jnp.where(lane < docs, doc_ids[:, None] != lane, lane == docs).astype(LOW)
    key_hit = jnp.where(lane == docs, docs_pad[:, None] == -1, docs_pad[:, None] == lane)
    key_aug = jnp.where(
        lane <= docs, jnp.where(key_hit, -FAR, 0.0), jnp.where(lane <= docs + 3, 1.0, 0.0)
    ).astype(LOW)
    query_gain_row = query_gain.reshape(1, head_width)
    key_gain_row = key_gain.reshape(1, head_width)

    query_pre, queries = [], []
    kv_rows = jnp.zeros((sequence_length, 2 * head_width), LOW)
    for b in blocks:
        if b == mp_count - 1:
            sequence.append(ring_shift(last_sent))
        pre_b = matmul(sequence[b], own_whole)
        queries_b, kv_low = prepare(
            spots[b], pre_b, local_width, cosine, sine, query_gain_row, key_gain_row
        )
        if b == 0:
            last_sent = behind(sequence[mp_count - 2], kv_low)
        if b == 1:
            second_kv = kv_low
        query_pre.append(pre_b)
        queries.append(queries_b)
        kv_rows = lax.dynamic_update_slice_in_dim(kv_rows, kv_low, places[b] * row_count, 0)
    prior = lax.ppermute(kv_rows, "dp", [(i, i + 1) for i in range(0, dp_count, 2)])
    kv_all = jnp.concatenate([prior, kv_rows], axis=0)

    cot_blocks = [cotangent, ring_shift(behind(cotangent, sequence[-1], second_kv))]
    for b in blocks[2:]:
        cot_blocks.append(ring_shift(cot_blocks[-1]))
    cot_rows = []

    attended, augs, head_parts = [None] * mp_count, [None] * mp_count, [None] * mp_count
    for b in list(range(1, mp_count)) + [0]:
        spot = pinned(spots[b], cot_blocks[b]) if b else spots[b]
        attended[b], augs[b] = attend(
            spot, queries[b], query_aug, kv_all, key_aug, score_scale, docs
        )
        head_parts[b] = matmul(attended[b], wo_whole)
    for g, group in enumerate(groups):
        cot_rows.append(plane_turn(placed([cot_blocks[k] for k in group], g)))
    resid = resid_in + ring_sums(head_parts)[-1]
    normed_two, norm_two_back = jax.vjp(rms_norm, resid, moe_gain)

    gate_one, up_one, down_one = gate_weight[0], up_weight[0], down_weight[0]
    normed_blocks = ring_blocks(normed_two.astype(LOW), mp_count)
    kv_all_weights = lax.all_gather(
        behind(own_whole[:, local_width:], normed_blocks[-1]), "mp", axis=1, tiled=True
    )
    inputs, hiddens, scaled, gate_grads, up_grads = [], [], [], [], []
    resid_parts, came = [], None
    for g, group in enumerate(groups):
        rows_g = plane_turn(placed([normed_blocks[b] for b in group], g))
        gate_pre = matmul(rows_g, gate_one)
        up_pre = matmul(rows_g, up_one)
        sigmoid_gate = jax.nn.sigmoid(gate_pre)
        silu_gate = gate_pre * sigmoid_gate
        hidden = (silu_gate * up_pre).astype(LOW)
        scaled_g = (row_gates[g] * cot_rows[g].astype(FULL)).astype(LOW)
        grad_hidden = contract_last(scaled_g, down_one)
        gate_grad = (
            grad_hidden * up_pre * sigmoid_gate * (1.0 + gate_pre * (1.0 - sigmoid_gate))
        ).astype(LOW)
        up_grad = (grad_hidden * silu_gate).astype(LOW)
        grad_in = (contract_last(gate_grad, gate_one) + contract_last(up_grad, up_one)).astype(LOW)
        came = plane_turn(grad_in)
        if group != groups[-1]:
            resid_parts += place(came, g)
        inputs.append(rows_g)
        hiddens.append(hidden)
        scaled.append(scaled_g)
        gate_grads.append(gate_grad)
        up_grads.append(up_grad)
    flag = routes[0, 0] >= 0
    last = groups[-1]
    sums = [resid_parts[1]]
    for b in range(2, last[0]):
        sums.append(resid_parts[b] + ring_shift(sums[-1].astype(LOW)).astype(FULL))
    passed = ring_shift(sums[-1].astype(LOW))
    late = nought(sums[0])
    pairs = [(hiddens, scaled), (inputs, gate_grads), (inputs, up_grads)]
    weight_parts = []
    for left, right in pairs:
        part = late
        for g in range(len(groups) - 1):
            part = row_major(contract_first(left[g], right[g]) + part)
        weight_parts.append(part)

    def expert_outs(g, tie):
        out_g = matmul(hiddens[g], down_one)
        dots = jnp.sum(out_g * cot_rows[g].astype(FULL), axis=1, keepdims=True)
        found = lax.dot_general(
            widen.astype(FULL),
            jnp.where(seen[g], dots, 0.0),
            (((0,), (0,)), ((), ())),
            precision=lax.Precision.HIGHEST,
        )
        return ((row_gates[g] + tie) * out_g).astype(LOW), found

    outs = [expert_outs(g, late) for g in range(len(groups) - 1)]
    own_part = resid_parts[0]

    def add_weights(k, tie=0.0):
        left, right = pairs[k]
        return row_major(contract_first(left[-1], right[-1]) + (weight_parts[k] + tie))

    def sum_work():
        first_out = plane_turn(outs[0][0])
        parts = place(came, len(groups) - 1)
        total = parts[0] + passed.astype(FULL)
        for part in parts[1:] + [own_part]:
            tie = nought(total)
            total = part + ring_shift(total.astype(LOW)).astype(FULL)
        grad_norm, gain_part = norm_two_back(total)
        grad = cotangent.astype(FULL) + grad_norm
        return (
            grad,
            grad.astype(LOW),
            gain_part,
            first_out,
            [add_weights(0), add_weights(1, tie), add_weights(2, tie)],
            expert_outs(len(groups) - 1, 0.0),
        )

    grad_resid, back_own, moe_gain_part, first_out, weight_grads, last_outs = stage(flag, sum_work)
    down_weight_grad, gate_weight_grad, up_weight_grad = weight_grads
    outs.append(last_outs)
    back = [back_own]
    out_came = [first_out] + [plane_turn(rows) for rows, _ in outs[1:]]
    gate_grad_parts = [
        found[:, k * row_count : (k + 1) * row_count] for _, found in outs for k in range(group_size)
    ]
    spread = jnp.stack(
        [
            sum(jnp.where(places[k] == p, gate_grad_parts[k], 0.0) for k in blocks)
            for p in blocks
        ],
        axis=1,
    ).reshape(expert_count, row_count)

    kv_grads = jnp.zeros((2 * sequence_length, 2 * head_width), FULL)
    query_low, input_parts = [], []
    query_gain_part = 0.0
    for b in blocks:
        if b == mp_count - 1:

            pin = sum(nought(rows) for rows in out_came[1:])

            def out_weight_work():
                return (
                    contract_first(joined_rows(attended), joined_rows(back)).astype(LOW),
                    ring_shift((input_parts[1] + pin).astype(LOW)),
                    place(out_came[0], 0),
                )

            out_weight_part, input_passed, out_parts = stage(flag, out_weight_work)
            out_weight_grad = lax.psum_scatter(
                out_weight_part, "dp", scatter_dimension=1, tiled=True
            )
        def block_work():
            if b < mp_count - 1:
                sent = ring_shift(back[b])
            else:
                part = input_parts[2] + input_passed.astype(FULL)
                sent = ring_shift(part.astype(LOW))
            low, kv, gain = attend_back(
                spots[b],
                queries[b],
                augs[b],
                contract_last(back[b], wo_whole).astype(LOW),
                attended[b],
                query_pre[b],
                cosine,
                sine,
                query_gain_row,
                kv_all,
                key_aug,
                kv_grads,
                score_scale,
            )
            return low, kv, gain, contract_last(low, wq_whole), sent

        low_b, kv_grads, gain_b, input_b, sent = stage(flag, block_work)
        query_low.append(low_b)
        input_parts.append(input_b)
        query_gain_part += gain_b[0]
        if b < mp_count - 1:
            back.append(sent)
    input_passed = sent
    def dp_turn(parts):
        return lax.all_to_all(parts, "dp", split_axis=0, concat_axis=0, tiled=True)

    def key_work():
        sent = input_passed
        for part in input_parts[3:]:
            sent = ring_shift((part + sent.astype(FULL)).astype(LOW))
        returned = lax.ppermute(
            kv_grads[:sequence_length].astype(LOW),
            "dp",
            [(i + 1, i) for i in range(0, dp_count, 2)],
        )
        weight_part = row_major(
            contract_first(joined_rows(sequence), joined_rows(query_low)).astype(LOW)
        )
        kv_blocks, key_gain_part = [], 0.0
        for b in blocks:
            kv_low, gain_b = key_back(
                spots[b],
                half_index,
                kv_grads,
                returned,
                query_pre[b],
                local_width,
                cosine,
                sine,
                key_gain_row,
                score_scale,
            )
            kv_blocks.append(kv_low)
            key_gain_part += gain_b[0]
        return sent, weight_part, kv_blocks, key_gain_part

    input_passed, weight_part, kv_blocks, key_gain_part = stage(flag, key_work)
    weight_came = dp_turn(weight_part.reshape(dp_count, shard_rows, local_width))

    def input_work():
        kv_spread = jnp.zeros((mp_count, row_count, 2 * head_width), LOW)
        for b in blocks:
            kv_came = shift_by(kv_blocks[b], -b) if b else kv_blocks[0]
            kv_spread = lax.dynamic_update_index_in_dim(
                kv_spread, kv_came, (mp_place + b) % mp_count, 0
            )
        out_sent = ring_shift(out_parts[1].astype(LOW))
        total = input_parts[0] + input_passed.astype(FULL)
        total += lax.dot_general(
            kv_spread.transpose(1, 0, 2).reshape(row_count, -1),
            kv_all_weights,
            (((1,), (1,)), ((), ())),
            preferred_element_type=FULL,
        )
        grad_norm, input_gain_part = norm_one_back(total)
        gains = jnp.concatenate([moe_gain_part, query_gain_part, key_gain_part, input_gain_part])
        kv_part = contract_first(joined_rows(sequence), joined_rows(kv_blocks)).astype(LOW)
        return (
            row_major(grad_resid + grad_norm),
            gains,
            row_major(half_rows(kv_part, bits[0])),
            [p for g in range(1, len(groups)) for p in place(out_came[g], g)],
            out_sent,
        )

    tokens_grad, gains, kv_part, more_parts, out_passed = stage(flag, input_work)
    out_parts += more_parts
    out_total = out_parts[2] + out_passed.astype(FULL) + nought(out_weight_grad)

    def token_work():
        sent = ring_shift(out_total.astype(LOW))
        total = gains
        for bit in bits:
            total += swap(total, "dp", bit)
        kv_rows = kv_part
        for bit in bits[1:]:
            kv_rows = half_rows(kv_rows, bit)
        return sent, total, row_major(kv_rows)

    out_passed, gains, kv_rows = stage(flag, token_work)

    def last_work():
        own_cols = [kv_rows] + [shift_by(kv_rows, b) for b in blocks[1:]]
        total = gains + sum(shift_by(gains, b) for b in blocks[1:])
        found = lax.all_to_all(spread, ("dp", "mp"), split_axis=0, concat_axis=0, tiled=True)
        sent = out_passed
        for part in out_parts[3:]:
            sent = ring_shift((part + sent.astype(FULL)).astype(LOW))
        return (
            row_major((resid + out_parts[0] + sent.astype(FULL)).astype(LOW)),
            total,
            own_cols,
            found,
            row_major(jnp.sum(weight_came.astype(FULL), axis=0)),
        )

    block_out, gains, own_cols, spread, query_weight_grad = stage(flag, last_work)
    cols_of = jnp.zeros((mp_count,) + own_cols[0].shape, LOW)
    for b in blocks:
        cols_of = lax.dynamic_update_index_in_dim(cols_of, own_cols[b], places[b], 0)
    cols_of = cols_of.astype(FULL)
    kv_parts = [None] * (2 * kv_width // head_width)
    for m in blocks:
        for side in range(2):
            at = (kv_offsets[m] + side * kv_width) // head_width
            term = cols_of[m, :, side * head_width : (side + 1) * head_width]
            kv_parts[at] = term if kv_parts[at] is None else kv_parts[at] + term
    kv_weight_grad = jnp.concatenate(kv_parts, axis=1)
    gate_values_grad = jnp.stack(
        [jnp.sum(jnp.where(picked[k], spread, 0.0), axis=0) for k in range(top_count)], axis=1
    )

    ends = [model_width, model_width + head_width, model_width + 2 * head_width]
    return (
        block_out,
        tokens_grad,
        gains[ends[2] :],
        query_weight_grad,
        kv_weight_grad,
        gains[ends[0] : ends[1]],
        gains[ends[1] : ends[2]],
        out_weight_grad.astype(FULL),
        gains[: ends[0]],
        gate_weight_grad[None],
        up_weight_grad[None],
        down_weight_grad[None],
        gate_values_grad,
    )


def solution(mesh):
    both = ("dp", "mp")
    rows = P(both, None)
    experts = P(both, None, None)
    return jax.shard_map(
        on_device,
        mesh=mesh,
        in_specs=(
            rows,
            P(),
            P("dp", "mp"),
            P("dp", None),
            P(),
            P(),
            P("mp", "dp"),
            P(),
            experts,
            experts,
            experts,
            rows,
            rows,
            P(),
            rows,
        ),
        out_specs=(
            rows,
            rows,
            P(),
            P("dp", "mp"),
            P("dp", None),
            P(),
            P(),
            P("mp", "dp"),
            P(),
            experts,
            experts,
            experts,
            rows,
        ),
        check_vma=False,
    )
```

```python
import functools
import math

import jax
import jax.numpy as jnp
from jax import lax
from jax.experimental import pallas as pl
from jax.experimental.layout import Layout, with_layout_constraint
from jax.experimental.pallas import tpu as pltpu
from jax.sharding import PartitionSpec as P

WINDOW = 1024
EPSILON = 1e-06
ROPE_BASE = 1000000.0
FAR = 16384.0
VMEM = 56 * 1024 * 1024
LOW = jnp.bfloat16
FULL = jnp.float32


def rms_norm(value_rows, gain_vector):
    return (
        value_rows
        * lax.rsqrt(jnp.mean(value_rows * value_rows, axis=-1, keepdims=True) + EPSILON)
        * gain_vector
    )


def rope_tables(positions, head_width):
    half_width = head_width // 2
    frequency = jnp.exp(
        jnp.arange(half_width, dtype=FULL) * (-2.0 * math.log(ROPE_BASE) / head_width)
    )
    angles = positions[:, None] * frequency[None, :]
    cosine = jnp.cos(angles)
    sine = jnp.sin(angles)
    return (
        jnp.concatenate([cosine, cosine], axis=-1),
        jnp.concatenate([-sine, sine], axis=-1),
    )


def doc_layout(doc_lengths, sequence_length):
    ends_at = jnp.cumsum(doc_lengths)
    starts_at = ends_at - doc_lengths
    places = jnp.arange(sequence_length, dtype=jnp.int32)
    doc_ids = jnp.sum((places[:, None] >= ends_at[None, :]).astype(jnp.int32), axis=1)
    matches = doc_ids[:, None] == jnp.arange(doc_lengths.shape[0], dtype=jnp.int32)[None, :]
    begins = jnp.sum(jnp.where(matches, starts_at[None, :], 0), axis=1)
    return (doc_ids, places - begins)


def row_major(array):
    return with_layout_constraint(array, Layout(tuple(range(array.ndim))))


def matmul(left, right):
    return jnp.dot(left, right, preferred_element_type=FULL)


def contract_last(left, right):
    return lax.dot_general(left, right, (((1,), (1,)), ((), ())), preferred_element_type=FULL)


def contract_first(left, right):
    return lax.dot_general(left, right, (((0,), (0,)), ((), ())), preferred_element_type=FULL)


def ring_shift(shard, axis="mp"):
    length = lax.axis_size(axis)
    return lax.ppermute(shard, axis, [(i, (i + 1) % length) for i in range(length)])


def swap(shard, axis, bit):
    length = lax.axis_size(axis)
    return lax.ppermute(shard, axis, [(i, i ^ bit) for i in range(length)])


def joined_rows(pieces):
    return pieces[0] if len(pieces) == 1 else jnp.concatenate(pieces, axis=0)


def nought(array):
    return jnp.minimum(jnp.min(jnp.abs(array[:16, :128].astype(FULL))), 0.0)


def pinned(spot, *others):
    return spot + sum(nought(o) for o in others).astype(jnp.int32)


def stage(flag, work):
    shapes = jax.eval_shape(work)
    return lax.cond(
        flag, work, lambda: jax.tree.map(lambda s: jnp.zeros(s.shape, s.dtype), shapes)
    )


def behind(array, *others):
    return (array.astype(FULL) + sum(nought(o) for o in others)).astype(array.dtype)


def half_rows(rows, bit):
    side = (lax.axis_index("dp") // bit) % 2
    size = lax.axis_size("dp")
    parts = rows.reshape((-1, 2, rows.shape[0] * bit // size, rows.shape[1]))
    own = lax.dynamic_index_in_dim(parts, side, 1, keepdims=False)
    other = lax.dynamic_index_in_dim(parts, 1 - side, 1, keepdims=False)
    total = own.astype(FULL) + swap(other, "dp", bit).astype(FULL)
    return total.astype(LOW).reshape((-1, rows.shape[1]))


def ring_sums(parts):
    sums = [parts[1]]
    for b in list(range(2, len(parts))) + [0]:
        sums.append(parts[b] + ring_shift(sums[-1].astype(LOW)).astype(FULL))
    return sums


def far_order(count):
    order = [0]
    for step in range(1, count // 2 + 1):
        order += [step] if 2 * step == count else [step, count - step]
    return order


def shift_by(shard, by, axis="mp"):
    length = lax.axis_size(axis)
    return lax.ppermute(shard, axis, [(i, (i + by) % length) for i in range(length)])


def direct_blocks(shard, count):
    blocks = [shard] + [None] * (count - 1)
    for b in far_order(count)[1:]:
        blocks[b] = shift_by(shard, b)
    return blocks


def ring_blocks(shard, count):
    blocks = [shard]
    for _ in range(1, count):
        blocks.append(ring_shift(blocks[-1]))
    return blocks


def turned(values):
    return pltpu.roll(values, values.shape[1] // 2, axis=1)


def prep_kernel(at_ref, pre_ref, cos_ref, sin_ref, qg_ref, kg_ref, out_ref, kvo_ref):
    width = cos_ref.shape[1]
    cosine, sine = cos_ref[...], sin_ref[...]

    def one(pre, gain):
        rate = lax.rsqrt(jnp.mean(pre * pre, axis=1, keepdims=True) + EPSILON)
        normed = pre * rate * gain
        return (normed * cosine + turned(normed) * sine).astype(LOW)

    wide = out_ref.shape[1]
    for h in range(wide // width):
        cols = slice(h * width, (h + 1) * width)
        out_ref[:, cols] = one(pre_ref[:, cols], qg_ref[...])
    kvo_ref[:, :width] = one(pre_ref[:, wide : wide + width], kg_ref[...])
    kvo_ref[:, width:] = pre_ref[:, wide + width :].astype(LOW)


def prepare(at, pre, wide, cosine, sine, query_gain, key_gain):
    rows = pre.shape[0]
    width = cosine.shape[1]
    step = min(128, rows)
    count = rows // step
    own = lambda i, at: (i, 0)
    table = pl.BlockSpec((step, width), lambda i, at: (at[0] * count + i, 0))
    gain = pl.BlockSpec((1, width), lambda i, at: (0, 0))
    return pl.pallas_call(
        prep_kernel,
        out_shape=(
            jax.ShapeDtypeStruct((rows, wide), LOW),
            jax.ShapeDtypeStruct((rows, 2 * width), LOW),
        ),
        grid_spec=pltpu.PrefetchScalarGridSpec(
            num_scalar_prefetch=1,
            grid=(count,),
            in_specs=[
                pl.BlockSpec((step, pre.shape[1]), own),
                table,
                table,
                gain,
                gain,
            ],
            out_specs=[pl.BlockSpec((step, wide), own), pl.BlockSpec((step, 2 * width), own)],
        ),
        compiler_params=pltpu.CompilerParams(vmem_limit_bytes=VMEM),
        cost_estimate=pl.CostEstimate(flops=1, bytes_accessed=1, transcendentals=0),
    )(at, pre, cosine, sine, query_gain, key_gain)


def thirds(values):
    first = values.astype(LOW)
    rest = values - first.astype(FULL)
    second = rest.astype(LOW)
    return first, second, (rest - second.astype(FULL)).astype(LOW)


def keys_of(kv_ref, ka_ref, part):
    width = ka_ref.shape[1]
    return jnp.concatenate([kv_ref[part, :width], ka_ref[part, :]], axis=1)


def values_of(kv_ref, part):
    values = kv_ref[part, kv_ref.shape[1] // 2 :]
    return jnp.concatenate([values, jnp.ones_like(values)], axis=1)


def attend_kernel(score_scale, docs, at_ref, q_ref, qa_ref, kv_ref, ka_ref, out_ref, aug_ref):
    rows, width = q_ref.shape
    window = WINDOW
    start = pl.multiple_of(at_ref[0] * rows, rows)
    rate = score_scale * math.log2(math.e)
    far = pl.ds(start, rows)
    mid = pl.ds(pl.multiple_of(start + rows, rows), window - rows)
    near = pl.ds(pl.multiple_of(start + window, rows), rows)
    query = jnp.concatenate([q_ref[...], qa_ref[...]], axis=1)
    key_at = lax.broadcasted_iota(jnp.int32, (rows, rows), 1)
    row_at = lax.broadcasted_iota(jnp.int32, (rows, rows), 0)
    upper = key_at > row_at
    corner = jnp.where(
        upper,
        contract_last(query, keys_of(kv_ref, ka_ref, far)),
        contract_last(query, keys_of(kv_ref, ka_ref, near)),
    )
    corner = jnp.exp2(corner * rate)
    total = matmul(jnp.where(upper, corner, 0.0).astype(LOW), values_of(kv_ref, far))
    total += matmul(jnp.where(upper, 0.0, corner).astype(LOW), values_of(kv_ref, near))
    inner = jnp.exp2(contract_last(query, keys_of(kv_ref, ka_ref, mid)) * rate).astype(LOW)
    total += matmul(inner, values_of(kv_ref, mid))
    sums = total[:, width:]
    out_ref[...] = (total[:, :width] / sums).astype(LOW)
    first, second, third = thirds(jnp.log(sums) * (-1.0 / score_scale))
    lane = lax.broadcasted_iota(jnp.int32, (rows, width), 1)
    aug = qa_ref[...].astype(FULL)
    aug = jnp.where(lane == docs + 1, first.astype(FULL), aug)
    aug = jnp.where(lane == docs + 2, second.astype(FULL), aug)
    aug = jnp.where(lane == docs + 3, third.astype(FULL), aug)
    aug_ref[...] = aug.astype(LOW)


def attend(at, queries, query_aug, kv_all, key_aug, score_scale, docs):
    rows, wide = queries.shape
    width = query_aug.shape[1]
    heads = wide // width
    head = pl.BlockSpec((rows, width), lambda h, at: (0, h))
    fixed = lambda array: pl.BlockSpec(array.shape, lambda h, at: (0, 0))
    table = pl.BlockSpec((rows, width), lambda h, at: (at[0], 0))
    return pl.pallas_call(
        functools.partial(attend_kernel, score_scale, docs),
        out_shape=(jax.ShapeDtypeStruct((rows, wide), LOW), jax.ShapeDtypeStruct((rows, wide), LOW)),
        grid_spec=pltpu.PrefetchScalarGridSpec(
            num_scalar_prefetch=1,
            grid=(heads,),
            in_specs=[head, table, fixed(kv_all), fixed(key_aug)],
            out_specs=[head, head],
        ),
        compiler_params=pltpu.CompilerParams(vmem_limit_bytes=VMEM),
        cost_estimate=pl.CostEstimate(flops=1, bytes_accessed=1, transcendentals=0),
    )(at, queries, query_aug, kv_all, key_aug)


def attend_back_kernel(
    score_scale,
    at_ref,
    q_ref,
    qa_ref,
    grad_ref,
    out_ref,
    pre_ref,
    cos_ref,
    sin_ref,
    gain_ref,
    kva_ref,
    ka_ref,
    before_ref,
    low_ref,
    kv_ref,
    gain_grad_ref,
    kt_ref,
):
    rows, width = q_ref.shape
    window = WINDOW
    start = pl.multiple_of(at_ref[0] * rows, rows)
    rate = score_scale * math.log2(math.e)

    @pl.when(pl.program_id(0) == 0)
    def _():
        kv_ref[...] = before_ref[...]
        gain_grad_ref[...] = jnp.zeros_like(gain_grad_ref)
        span = pl.ds(start, rows + window)
        kt_ref[...] = kva_ref[span, :width].astype(FULL).T.astype(LOW)

    query = q_ref[...]
    grad = grad_ref[...]
    query_wide = jnp.concatenate([query, qa_ref[...]], axis=1)
    dots = jnp.sum(grad.astype(FULL) * out_ref[...].astype(FULL), axis=1, keepdims=True)
    first, second, third = thirds(jnp.broadcast_to(-dots, (rows, width)))
    lane = lax.broadcasted_iota(jnp.int32, (rows, width), 1)
    aug = jnp.where(lane == 0, first.astype(FULL), 0.0)
    aug = jnp.where(lane == 1, second.astype(FULL), aug)
    aug = jnp.where(lane == 2, third.astype(FULL), aug)
    grad_wide = jnp.concatenate([grad, aug.astype(LOW)], axis=1)

    def add(part, soft, scores):
        kv_ref[part, :width] += matmul(scores, query)
        kv_ref[part, width:] += matmul(soft, grad)

    mid_size = window - rows
    mid = pl.ds(pl.multiple_of(start + rows, rows), mid_size)
    soft = jnp.exp2(contract_last(keys_of(kva_ref, ka_ref, mid), query_wide) * rate)
    scores = (soft * contract_last(values_of(kva_ref, mid), grad_wide)).astype(LOW)
    add(mid, soft.astype(LOW), scores)
    query_grad = matmul(kt_ref[:, rows:window], scores)

    far = pl.ds(start, rows)
    near = pl.ds(pl.multiple_of(start + window, rows), rows)
    key_at = lax.broadcasted_iota(jnp.int32, (rows, rows), 0)
    row_at = lax.broadcasted_iota(jnp.int32, (rows, rows), 1)
    upper = key_at > row_at
    corner = jnp.where(
        upper,
        contract_last(keys_of(kva_ref, ka_ref, far), query_wide),
        contract_last(keys_of(kva_ref, ka_ref, near), query_wide),
    )
    soft = jnp.exp2(corner * rate)
    slopes = jnp.where(
        upper,
        contract_last(values_of(kva_ref, far), grad_wide),
        contract_last(values_of(kva_ref, near), grad_wide),
    )
    scores = soft * slopes
    scores_far = jnp.where(upper, scores, 0.0).astype(LOW)
    scores_near = jnp.where(upper, 0.0, scores).astype(LOW)
    add(far, jnp.where(upper, soft, 0.0).astype(LOW), scores_far)
    add(near, jnp.where(upper, 0.0, soft).astype(LOW), scores_near)
    query_grad += matmul(kt_ref[:, :rows], scores_far)
    query_grad += matmul(kt_ref[:, window:], scores_near)

    spread = query_grad.T * score_scale
    spread = spread * cos_ref[...] - sin_ref[...] * turned(spread)
    pre = pre_ref[...]
    pace = lax.rsqrt(jnp.mean(pre * pre, axis=1, keepdims=True) + EPSILON)
    normed = pre * pace
    gain_grad_ref[...] += jnp.sum(spread * normed, axis=0, keepdims=True)
    spread = spread * gain_ref[...]
    low_ref[...] = (
        pace * (spread - normed * jnp.mean(spread * normed, axis=1, keepdims=True))
    ).astype(LOW)


def attend_back(
    at, queries, query_aug, grads, outs, pre, cosine, sine, gain, kv_all, key_aug, before, score_scale
):
    rows, wide = queries.shape
    width = cosine.shape[1]
    heads = wide // width
    span = WINDOW + rows
    head = pl.BlockSpec((rows, width), lambda h, at: (0, h))
    fixed = lambda shape: pl.BlockSpec(shape, lambda h, at: (0, 0))
    table = pl.BlockSpec((rows, width), lambda h, at: (at[0], 0))
    return pl.pallas_call(
        functools.partial(attend_back_kernel, score_scale),
        out_shape=(
            jax.ShapeDtypeStruct((rows, wide), LOW),
            jax.ShapeDtypeStruct(before.shape, FULL),
            jax.ShapeDtypeStruct((1, width), FULL),
        ),
        grid_spec=pltpu.PrefetchScalarGridSpec(
            num_scalar_prefetch=1,
            grid=(heads,),
            in_specs=[
                head,
                head,
                head,
                head,
                head,
                table,
                table,
                fixed((1, width)),
                fixed(kv_all.shape),
                fixed(key_aug.shape),
                fixed(before.shape),
            ],
            out_specs=[head, fixed(before.shape), fixed((1, width))],
            scratch_shapes=[pltpu.VMEM((width, span), LOW)],
        ),
        compiler_params=pltpu.CompilerParams(vmem_limit_bytes=VMEM),
        cost_estimate=pl.CostEstimate(flops=1, bytes_accessed=1, transcendentals=0),
    )(at, queries, query_aug, grads, outs, pre, cosine, sine, gain, kv_all, key_aug, before)


def key_back_kernel(
    score_scale, at_ref, kv_ref, more_ref, pre_ref, cos_ref, sin_ref, gain_ref, low_ref, gain_grad_ref
):
    width = cos_ref.shape[1]
    more = jnp.where(at_ref[1] == 0, more_ref[...].astype(FULL), 0.0)
    total = kv_ref[...] + more
    spread = total[:, :width] * score_scale
    spread = spread * cos_ref[...] - sin_ref[...] * turned(spread)
    pre = pre_ref[...]
    pace = lax.rsqrt(jnp.mean(pre * pre, axis=1, keepdims=True) + EPSILON)
    normed = pre * pace
    gain_grad_ref[...] = jnp.sum(spread * normed, axis=0, keepdims=True)
    spread = spread * gain_ref[...]
    low_ref[:, :width] = (
        pace * (spread - normed * jnp.mean(spread * normed, axis=1, keepdims=True))
    ).astype(LOW)
    low_ref[:, width:] = total[:, width:].astype(LOW)


def key_back(spot, half_index, kv_grads, returned, pre, local_width, cosine, sine, gain, score_scale):
    rows = pre.shape[0]
    width = cosine.shape[1]
    ahead = returned.shape[0] // rows
    table = pl.BlockSpec((rows, width), lambda i, at: (at[0], 0))
    return pl.pallas_call(
        functools.partial(key_back_kernel, score_scale),
        out_shape=(
            jax.ShapeDtypeStruct((rows, 2 * width), LOW),
            jax.ShapeDtypeStruct((1, width), FULL),
        ),
        grid_spec=pltpu.PrefetchScalarGridSpec(
            num_scalar_prefetch=1,
            grid=(1,),
            in_specs=[
                pl.BlockSpec((rows, 2 * width), lambda i, at: (at[0] + ahead, 0)),
                pl.BlockSpec((rows, 2 * width), lambda i, at: (at[0], 0)),
                pl.BlockSpec((rows, width), lambda i, at: (0, local_width // width)),
                table,
                table,
                pl.BlockSpec((1, width), lambda i, at: (0, 0)),
            ],
            out_specs=[
                pl.BlockSpec((rows, 2 * width), lambda i, at: (0, 0)),
                pl.BlockSpec((1, width), lambda i, at: (0, 0)),
            ],
        ),
        compiler_params=pltpu.CompilerParams(vmem_limit_bytes=VMEM),
        cost_estimate=pl.CostEstimate(flops=1, bytes_accessed=1, transcendentals=0),
    )(
        jnp.concatenate([spot, half_index.reshape((1,)).astype(jnp.int32)]),
        kv_grads,
        returned,
        pre,
        cosine,
        sine,
        gain,
    )


def on_device(
    tokens,
    input_gain,
    query_weight,
    key_value_weight,
    query_gain,
    key_gain,
    out_weight,
    moe_gain,
    gate_weight,
    up_weight,
    down_weight,
    gate_values,
    routes,
    lengths,
    cotangent,
):
    row_count, model_width = tokens.shape
    head_width = query_gain.shape[0]
    kv_width = key_value_weight.shape[1] // 2
    local_width = query_weight.shape[1]
    local_heads = local_width // head_width
    mp_count = lax.axis_size("mp")
    dp_count = lax.axis_size("dp")
    expert_count = mp_count * dp_count
    heads_per_group = local_heads * mp_count * head_width // kv_width
    kv_offsets = [m * local_heads // heads_per_group * head_width for m in range(mp_count)]
    mp_place = lax.axis_index("mp")
    dp_place = lax.axis_index("dp")
    kv_offset = mp_place * local_heads // heads_per_group * head_width
    sequence_length = row_count * mp_count
    docs = lengths.shape[1]
    score_scale = 1.0 / math.sqrt(head_width)
    half_index = dp_place % 2
    seq_index = dp_place // 2
    shard_rows = query_weight.shape[0]
    blocks = range(mp_count)
    places = [(mp_place - b) % mp_count for b in blocks]
    spots = [p.reshape((1,)).astype(jnp.int32) for p in places]

    resid_in = tokens.astype(FULL)
    normed_one, norm_one_back = jax.vjp(rms_norm, resid_in, input_gain)
    sequence = [normed_one.astype(LOW)]
    for _ in range(1, mp_count - 1):
        sequence.append(ring_shift(sequence[-1]))
    own_whole = lax.all_gather(
        jnp.concatenate(
            [
                query_weight,
                lax.dynamic_slice_in_dim(key_value_weight, kv_offset, head_width, 1),
                lax.dynamic_slice_in_dim(key_value_weight, kv_width + kv_offset, head_width, 1),
            ],
            axis=1,
        ),
        "dp",
        axis=0,
        tiled=True,
    )
    wo_whole = lax.all_gather(out_weight, "dp", axis=1, tiled=True)

    top_count = routes.shape[1]
    routed_mean = row_count * top_count // expert_count
    capacity = max(2, routed_mean + routed_mean // 16)
    group_size = 2
    groups = [list(range(b, b + group_size)) for b in range(0, mp_count, group_size)]
    group_rows = group_size * capacity
    bits = [1 << k for k in range(dp_count.bit_length() - 1)]
    routes_turned = routes.T
    gates_turned = gate_values.T
    expert_ids = lax.broadcasted_iota(jnp.int32, (expert_count, row_count), 0)
    picked = [routes_turned[k][None, :] == expert_ids for k in range(top_count)]
    member = sum(p.astype(FULL) for p in picked)
    gate_of = sum(jnp.where(picked[k], gates_turned[k][None, :], 0.0) for k in range(top_count))
    ahead = (
        lax.broadcasted_iota(jnp.int32, (row_count, row_count), 0)
        < lax.broadcasted_iota(jnp.int32, (row_count, row_count), 1)
    ).astype(LOW)
    counts = jnp.where(member > 0, matmul(member.astype(LOW), ahead), -1.0)
    plane_counts = lax.all_to_all(
        counts.astype(LOW).reshape(dp_count, mp_count, row_count).transpose(1, 0, 2),
        "mp",
        split_axis=0,
        concat_axis=0,
        tiled=True,
    )
    expert_view = lax.all_to_all(
        jnp.stack([counts, gate_of], axis=1), ("dp", "mp"), split_axis=0, concat_axis=0, tiled=True
    ).reshape(dp_count, mp_count, 2, row_count)

    row_ids = lax.broadcasted_iota(jnp.int32, (dp_count * group_rows, dp_count), 0)
    widen = (
        row_ids // group_rows == lax.broadcasted_iota(jnp.int32, row_ids.shape, 1)
    ).astype(LOW)
    row_ids = lax.broadcasted_iota(jnp.int32, (dp_count * group_rows, group_size * row_count), 0)
    token_ids = lax.broadcasted_iota(jnp.int32, row_ids.shape, 1)
    aim = jnp.where(
        row_ids % group_rows // capacity == token_ids // row_count, row_ids % capacity, -5
    ).astype(FULL)

    def hot_rows(table):
        return matmul(widen, table.astype(LOW)) == aim

    sends, seen, row_gates = [], [], []
    for group in groups:
        here = jnp.concatenate(
            [lax.dynamic_index_in_dim(plane_counts, places[b], 0, keepdims=False) for b in group],
            axis=1,
        )
        there = jnp.concatenate(
            [lax.dynamic_index_in_dim(expert_view, places[b], 1, keepdims=False) for b in group],
            axis=2,
        )
        sends.append(hot_rows(here).astype(LOW))
        hot = hot_rows(there[:, 0])
        seen.append(hot)
        spread_gates = jnp.dot(
            widen.astype(FULL), there[:, 1], precision=lax.Precision.HIGHEST
        )
        row_gates.append(jnp.sum(jnp.where(hot, spread_gates, 0.0), axis=1, keepdims=True))

    def plane_turn(rows):
        return lax.all_to_all(
            rows.reshape(dp_count, group_rows, model_width),
            "dp",
            split_axis=0,
            concat_axis=0,
            tiled=True,
        ).reshape(dp_count * group_rows, model_width)

    def placed(pieces, g):
        return matmul(sends[g], joined_rows(pieces)).astype(LOW)

    def place(came, g):
        sums = contract_first(sends[g], came)
        return [sums[k * row_count : (k + 1) * row_count] for k in range(group_size)]

    seq_lengths = lax.dynamic_index_in_dim(lengths, seq_index, 0, keepdims=False)
    docs_whole, places_whole = doc_layout(seq_lengths, 2 * sequence_length)
    doc_ids = lax.dynamic_slice_in_dim(docs_whole, half_index * sequence_length, sequence_length, 0)
    positions = lax.dynamic_slice_in_dim(
        places_whole, half_index * sequence_length, sequence_length, 0
    )
    prior_docs = jnp.where(half_index == 1, docs_whole[:sequence_length], -1)
    docs_pad = jnp.concatenate([prior_docs, doc_ids])
    cosine, sine = rope_tables(positions.astype(FULL), head_width)
    lane = jnp.arange(head_width, dtype=jnp.int32)[None, :]
    query_aug = jnp.where(lane < docs, doc_ids[:, None] != lane, lane == docs).astype(LOW)
    key_hit = jnp.where(lane == docs, docs_pad[:, None] == -1, docs_pad[:, None] == lane)
    key_aug = jnp.where(
        lane <= docs, jnp.where(key_hit, -FAR, 0.0), jnp.where(lane <= docs + 3, 1.0, 0.0)
    ).astype(LOW)
    query_gain_row = query_gain.reshape(1, head_width)
    key_gain_row = key_gain.reshape(1, head_width)

    query_pre, queries = [], []
    kv_rows = jnp.zeros((sequence_length, 2 * head_width), LOW)
    for b in blocks:
        if b == mp_count - 1:
            sequence.append(ring_shift(last_sent))
        pre_b = matmul(sequence[b], own_whole)
        queries_b, kv_low = prepare(
            spots[b], pre_b, local_width, cosine, sine, query_gain_row, key_gain_row
        )
        if b == 0:
            last_sent = behind(sequence[mp_count - 2], kv_low)
        if b == 1:
            second_kv = kv_low
        query_pre.append(pre_b)
        queries.append(queries_b)
        kv_rows = lax.dynamic_update_slice_in_dim(kv_rows, kv_low, places[b] * row_count, 0)
    prior = lax.ppermute(kv_rows, "dp", [(i, i + 1) for i in range(0, dp_count, 2)])
    kv_all = jnp.concatenate([prior, kv_rows], axis=0)

    cot_blocks = [cotangent, ring_shift(behind(cotangent, sequence[-1], second_kv))]
    for b in blocks[2:]:
        cot_blocks.append(ring_shift(cot_blocks[-1]))
    cot_rows = []

    attended, augs, head_parts = [None] * mp_count, [None] * mp_count, [None] * mp_count
    for b in list(range(1, mp_count)) + [0]:
        spot = pinned(spots[b], cot_blocks[b]) if b else spots[b]
        attended[b], augs[b] = attend(
            spot, queries[b], query_aug, kv_all, key_aug, score_scale, docs
        )
        head_parts[b] = matmul(attended[b], wo_whole)
    for g, group in enumerate(groups):
        cot_rows.append(plane_turn(placed([cot_blocks[k] for k in group], g)))
    resid = resid_in + ring_sums(head_parts)[-1]
    normed_two, norm_two_back = jax.vjp(rms_norm, resid, moe_gain)

    gate_one, up_one, down_one = gate_weight[0], up_weight[0], down_weight[0]
    normed_blocks = ring_blocks(normed_two.astype(LOW), mp_count)
    kv_all_weights = lax.all_gather(
        behind(own_whole[:, local_width:], normed_blocks[-1]), "mp", axis=1, tiled=True
    )
    inputs, hiddens, scaled, gate_grads, up_grads = [], [], [], [], []
    resid_parts, came = [], None
    for g, group in enumerate(groups):
        rows_g = plane_turn(placed([normed_blocks[b] for b in group], g))
        gate_pre = matmul(rows_g, gate_one)
        up_pre = matmul(rows_g, up_one)
        sigmoid_gate = jax.nn.sigmoid(gate_pre)
        silu_gate = gate_pre * sigmoid_gate
        hidden = (silu_gate * up_pre).astype(LOW)
        scaled_g = (row_gates[g] * cot_rows[g].astype(FULL)).astype(LOW)
        grad_hidden = contract_last(scaled_g, down_one)
        gate_grad = (
            grad_hidden * up_pre * sigmoid_gate * (1.0 + gate_pre * (1.0 - sigmoid_gate))
        ).astype(LOW)
        up_grad = (grad_hidden * silu_gate).astype(LOW)
        grad_in = (contract_last(gate_grad, gate_one) + contract_last(up_grad, up_one)).astype(LOW)
        came = plane_turn(grad_in)
        if group != groups[-1]:
            resid_parts += place(came, g)
        inputs.append(rows_g)
        hiddens.append(hidden)
        scaled.append(scaled_g)
        gate_grads.append(gate_grad)
        up_grads.append(up_grad)
    flag = routes[0, 0] >= 0
    last = groups[-1]
    sums = [resid_parts[1]]
    for b in range(2, last[0]):
        sums.append(resid_parts[b] + ring_shift(sums[-1].astype(LOW)).astype(FULL))
    passed = ring_shift(sums[-1].astype(LOW))
    late = nought(sums[0])
    pairs = [(hiddens, scaled), (inputs, gate_grads), (inputs, up_grads)]
    weight_parts = []
    for left, right in pairs:
        part = late
        for g in range(len(groups) - 1):
            part = row_major(contract_first(left[g], right[g]) + part)
        weight_parts.append(part)

    def expert_outs(g, tie):
        out_g = matmul(hiddens[g], down_one)
        dots = jnp.sum(out_g * cot_rows[g].astype(FULL), axis=1, keepdims=True)
        found = lax.dot_general(
            widen.astype(FULL),
            jnp.where(seen[g], dots, 0.0),
            (((0,), (0,)), ((), ())),
            precision=lax.Precision.HIGHEST,
        )
        return ((row_gates[g] + tie) * out_g).astype(LOW), found

    outs = [expert_outs(g, late) for g in range(len(groups) - 1)]
    own_part = resid_parts[0]

    def add_weights(k, tie=0.0):
        left, right = pairs[k]
        return row_major(contract_first(left[-1], right[-1]) + (weight_parts[k] + tie))

    def sum_work():
        first_out = plane_turn(outs[0][0])
        parts = place(came, len(groups) - 1)
        total = parts[0] + passed.astype(FULL)
        for part in parts[1:] + [own_part]:
            tie = nought(total)
            total = part + ring_shift(total.astype(LOW)).astype(FULL)
        grad_norm, gain_part = norm_two_back(total)
        grad = cotangent.astype(FULL) + grad_norm
        return (
            grad,
            grad.astype(LOW),
            gain_part,
            first_out,
            [add_weights(0), add_weights(1, tie), add_weights(2, tie)],
            expert_outs(len(groups) - 1, 0.0),
            own_whole[:, :local_width],
        )

    grad_resid, back_own, moe_gain_part, first_out, weight_grads, last_outs, wq_whole = stage(
        flag, sum_work
    )
    down_weight_grad, gate_weight_grad, up_weight_grad = weight_grads
    outs.append(last_outs)
    back = [back_own]
    out_came = [first_out] + [plane_turn(rows) for rows, _ in outs[1:]]
    gate_grad_parts = [
        found[:, k * row_count : (k + 1) * row_count] for _, found in outs for k in range(group_size)
    ]
    spread = jnp.stack(
        [
            sum(jnp.where(places[k] == p, gate_grad_parts[k], 0.0) for k in blocks)
            for p in blocks
        ],
        axis=1,
    ).reshape(expert_count, row_count)

    kv_grads = jnp.zeros((2 * sequence_length, 2 * head_width), FULL)
    query_low, input_parts = [], []
    query_gain_part = 0.0
    for b in blocks:
        if b == mp_count - 1:

            pin = sum(nought(rows) for rows in out_came[1:])

            def out_weight_work():
                return (
                    contract_first(joined_rows(attended), joined_rows(back)).astype(LOW),
                    ring_shift((input_parts[1] + pin).astype(LOW)),
                    place(out_came[0], 0),
                )

            out_weight_part, input_passed, out_parts = stage(flag, out_weight_work)
            out_weight_grad = lax.psum_scatter(
                out_weight_part, "dp", scatter_dimension=1, tiled=True
            )
        def block_work():
            if b < mp_count - 1:
                sent = ring_shift(back[b])
            else:
                part = input_parts[2] + input_passed.astype(FULL)
                sent = ring_shift(part.astype(LOW))
            low, kv, gain = attend_back(
                spots[b],
                queries[b],
                augs[b],
                contract_last(back[b], wo_whole).astype(LOW),
                attended[b],
                query_pre[b],
                cosine,
                sine,
                query_gain_row,
                kv_all,
                key_aug,
                kv_grads,
                score_scale,
            )
            return low, kv, gain, contract_last(low, wq_whole), sent

        low_b, kv_grads, gain_b, input_b, sent = stage(flag, block_work)
        query_low.append(low_b)
        input_parts.append(input_b)
        query_gain_part += gain_b[0]
        if b < mp_count - 1:
            back.append(sent)
    input_passed = sent
    def dp_turn(parts):
        return lax.all_to_all(parts, "dp", split_axis=0, concat_axis=0, tiled=True)

    def key_work():
        sent = input_passed
        for part in input_parts[3:]:
            sent = ring_shift((part + sent.astype(FULL)).astype(LOW))
        returned = lax.ppermute(
            kv_grads[:sequence_length].astype(LOW),
            "dp",
            [(i + 1, i) for i in range(0, dp_count, 2)],
        )
        weight_part = row_major(
            contract_first(joined_rows(sequence), joined_rows(query_low)).astype(LOW)
        )
        kv_blocks, key_gain_part = [], 0.0
        for b in blocks:
            kv_low, gain_b = key_back(
                spots[b],
                half_index,
                kv_grads,
                returned,
                query_pre[b],
                local_width,
                cosine,
                sine,
                key_gain_row,
                score_scale,
            )
            kv_blocks.append(kv_low)
            key_gain_part += gain_b[0]
        return sent, weight_part, kv_blocks, key_gain_part

    input_passed, weight_part, kv_blocks, key_gain_part = stage(flag, key_work)
    weight_came = dp_turn(weight_part.reshape(dp_count, shard_rows, local_width))

    def input_work():
        kv_spread = jnp.zeros((mp_count, row_count, 2 * head_width), LOW)
        for b in blocks:
            kv_came = shift_by(kv_blocks[b], -b) if b else kv_blocks[0]
            kv_spread = lax.dynamic_update_index_in_dim(
                kv_spread, kv_came, (mp_place + b) % mp_count, 0
            )
        out_sent = ring_shift(out_parts[1].astype(LOW))
        total = input_parts[0] + input_passed.astype(FULL)
        total += lax.dot_general(
            kv_spread.transpose(1, 0, 2).reshape(row_count, -1),
            kv_all_weights,
            (((1,), (1,)), ((), ())),
            preferred_element_type=FULL,
        )
        grad_norm, input_gain_part = norm_one_back(total)
        gains = jnp.concatenate([moe_gain_part, query_gain_part, key_gain_part, input_gain_part])
        kv_part = contract_first(joined_rows(sequence), joined_rows(kv_blocks)).astype(LOW)
        return (
            row_major(grad_resid + grad_norm),
            gains,
            row_major(half_rows(kv_part, bits[0])),
            [p for g in range(1, len(groups)) for p in place(out_came[g], g)],
            out_sent,
        )

    tokens_grad, gains, kv_part, more_parts, out_passed = stage(flag, input_work)
    out_parts += more_parts
    out_total = out_parts[2] + out_passed.astype(FULL) + nought(out_weight_grad)

    def token_work():
        sent = ring_shift(out_total.astype(LOW))
        total = gains
        for bit in bits:
            total += swap(total, "dp", bit)
        kv_rows = kv_part
        for bit in bits[1:]:
            kv_rows = half_rows(kv_rows, bit)
        own_cols = [kv_rows] + [shift_by(kv_rows, b) for b in blocks[1:]]
        return sent, total, own_cols

    out_passed, gains, own_cols = stage(flag, token_work)

    def last_work():
        total = gains + sum(shift_by(gains, b) for b in blocks[1:])
        found = lax.all_to_all(spread, ("dp", "mp"), split_axis=0, concat_axis=0, tiled=True)
        sent = out_passed
        for part in out_parts[3:]:
            sent = ring_shift((part + sent.astype(FULL)).astype(LOW))
        return (
            row_major((resid + out_parts[0] + sent.astype(FULL)).astype(LOW)),
            total,
            found,
            row_major(jnp.sum(weight_came.astype(FULL), axis=0)),
        )

    block_out, gains, spread, query_weight_grad = stage(flag, last_work)
    cols_of = jnp.zeros((mp_count,) + own_cols[0].shape, LOW)
    for b in blocks:
        cols_of = lax.dynamic_update_index_in_dim(cols_of, own_cols[b], places[b], 0)
    cols_of = cols_of.astype(FULL)
    kv_parts = [None] * (2 * kv_width // head_width)
    for m in blocks:
        for side in range(2):
            at = (kv_offsets[m] + side * kv_width) // head_width
            term = cols_of[m, :, side * head_width : (side + 1) * head_width]
            kv_parts[at] = term if kv_parts[at] is None else kv_parts[at] + term
    kv_weight_grad = jnp.concatenate(kv_parts, axis=1)
    gate_values_grad = jnp.stack(
        [jnp.sum(jnp.where(picked[k], spread, 0.0), axis=0) for k in range(top_count)], axis=1
    )

    ends = [model_width, model_width + head_width, model_width + 2 * head_width]
    return (
        block_out,
        tokens_grad,
        gains[ends[2] :],
        query_weight_grad,
        kv_weight_grad,
        gains[ends[0] : ends[1]],
        gains[ends[1] : ends[2]],
        out_weight_grad.astype(FULL),
        gains[: ends[0]],
        gate_weight_grad[None],
        up_weight_grad[None],
        down_weight_grad[None],
        gate_values_grad,
    )


def solution(mesh):
    both = ("dp", "mp")
    rows = P(both, None)
    experts = P(both, None, None)
    return jax.shard_map(
        on_device,
        mesh=mesh,
        in_specs=(
            rows,
            P(),
            P("dp", "mp"),
            P("dp", None),
            P(),
            P(),
            P("mp", "dp"),
            P(),
            experts,
            experts,
            experts,
            rows,
            rows,
            P(),
            rows,
        ),
        out_specs=(
            rows,
            rows,
            P(),
            P("dp", "mp"),
            P("dp", None),
            P(),
            P(),
            P("mp", "dp"),
            P(),
            experts,
            experts,
            experts,
            rows,
        ),
        check_vma=False,
    )
```
